256 devices in a mesh: blk: 32 (over z, y_lo, core), dp: 8 (over x, y_hi).
Axes of the slice: x: 4, y: 4 (y_hi: 2, y_lo: 2; y = y_hi * 2 + y_lo), z: 8, core: 2. Of those that a mesh axis runs over, the one named last changes fastest.
Arguments:
- images: bfloat16 [131072, 1152], P(('blk', 'dp')), may hold values from -4 to 4
- texts: bfloat16 [131072, 1152], P(('blk', 'dp')), may hold values from -4 to 4
- positives: int32 [256, 512], P(('blk', 'dp')), may hold values from 0 to 511, as said below
- log_scale: float32 [1], replicated, may hold values from 2.08 to 2.48
- bias: float32 [1], replicated, may hold values from -9 to -7
Outputs:
- image_grad: bfloat16 [131072, 1152], P(('blk', 'dp'))
- text_grad: bfloat16 [131072, 1152], P(('blk', 'dp'))
- totals: float32 [3], replicated
The draws below stay inside these ranges and needn't reach their ends.
Inputs may be any that keep to these rules, and one draw needn't show every extreme that they name: `positives`: each row orders 0 to 511, each once.
All inputs are finite; a program needn't handle non-finite values.
Results may differ from the reference program's by a relative error of at most 0.0056.
Values may be sent and summed in bfloat16 or wider, within the bound.
A program may use at most 64 MiB of HBM per device.

```python
import math
import jax
import jax.numpy as jnp
from jax import lax

D = 1152
LOCAL = 512
STEPS = 4
SHARDS = 256
IMAGES = 131072
N_BLK = 32
N_DP = 8


def block_levels():
    table = jnp.array([0.2, 0.3, 0.45, 0.6, 0.6, 0.45, 0.3, 0.2], jnp.float32)
    shard = jnp.arange(IMAGES, dtype=jnp.int32) // LOCAL
    position = shard // N_DP % 8
    return jnp.take(table, position)[:, None]


def shared_parts(key):
    key_perm, key_latent, key_common, key_weight = jax.random.split(key, 4)
    perm_keys = jax.random.split(key_perm, SHARDS)
    orders = jax.vmap(lambda k: jax.random.permutation(k, LOCAL))(perm_keys).astype(jnp.int32)
    latent = jax.random.normal(key_latent, (IMAGES, D), jnp.float32) / math.sqrt(D)
    common = jax.random.normal(key_common, (D,), jnp.float32) / math.sqrt(D)
    weights = jax.random.uniform(key_weight, (IMAGES, 1), jnp.float32, 0.85, 1.15) * block_levels()
    return (orders, latent, common, weights)


def noise_rows(key):
    key_noise = jax.random.fold_in(key, 0)
    noise = jax.random.normal(key_noise, (IMAGES, D), jnp.float32) / math.sqrt(D)
    return noise


def draw_positives(key, part):
    orders, latent, common, weights = shared_parts(key)
    return orders


def draw_images(key, part):
    orders, latent, common, weights = shared_parts(key)
    key = jax.random.fold_in(key, 11)
    key_noise, key_jitter = jax.random.split(key)
    shard = jnp.arange(IMAGES, dtype=jnp.int32) // LOCAL
    along_blk = (shard // N_DP).astype(jnp.float32) / max(N_BLK - 1, 1)
    along_dp = (shard % N_DP).astype(jnp.float32) / max(N_DP - 1, 1)
    level = 0.05 + 0.6 * along_blk + 0.3 * along_dp
    jitter = jax.random.uniform(key_jitter, (IMAGES,), jnp.float32, 0.8, 1.0)
    align = (level * jitter)[:, None]
    noise = noise_rows(key_noise)
    rows = weights * common[None, :] + align * latent + jnp.sqrt(1.0 - align * align) * noise
    return jnp.clip(rows, -4.0, 4.0).astype(jnp.bfloat16)


def draw_texts(key, part):
    orders, latent, common, weights = shared_parts(key)
    key = jax.random.fold_in(key, 23)
    inverse = jnp.argsort(orders, axis=1).astype(jnp.int32)
    blocks = latent.reshape(SHARDS, LOCAL, D)
    placed = jnp.take_along_axis(blocks, inverse[:, :, None], axis=1).reshape(IMAGES, D)
    placed_weights = jnp.take_along_axis(weights.reshape(SHARDS, LOCAL), inverse, axis=1).reshape(IMAGES, 1)
    noise = noise_rows(key)
    rows = placed_weights * common[None, :] + placed + 0.5 * noise
    return jnp.clip(rows, -4.0, 4.0).astype(jnp.bfloat16)


def setup_inputs(seed: int = 0) -> dict:
    splits = jax.random.split(jax.random.key(seed), 6)
    images = draw_images(jax.random.fold_in(splits[5], 71), 0)
    texts = draw_texts(jax.random.fold_in(splits[5], 71), 0)
    positives = draw_positives(jax.random.fold_in(splits[5], 71), 0)
    log_scale = jnp.clip(jax.random.uniform(splits[3], (1,), jnp.float32, 2.08, 2.48), 2.08, 2.48)
    bias = jnp.clip(jax.random.uniform(splits[4], (1,), jnp.float32, -9.0, -7.0), -9.0, -7.0)
    return {"images": images, "texts": texts, "positives": positives, "log_scale": log_scale, "bias": bias}


def normalize(raw):
    full = raw.astype(jnp.float32)
    factor = lax.rsqrt(lax.optimization_barrier(jnp.sum(full * full, axis=-1, keepdims=True)) + 1e-06)
    return (full * factor, factor)

def backnorm(grad, unit, factor):
    return factor * (grad - unit * lax.optimization_barrier(jnp.sum(unit * grad, axis=-1, keepdims=True)))

def reference(images, texts, positives, log_scale, bias):
    scale = jnp.exp(log_scale[0])
    shift = bias[0]
    x_full, x_factor = normalize(images.reshape(N_BLK, N_DP, LOCAL, D))
    y_full, y_factor = normalize(texts.reshape(N_BLK, N_DP, LOCAL, D))
    x_half = x_full.astype(jnp.bfloat16)
    y_half = y_full.astype(jnp.bfloat16)
    pairs = positives.reshape(N_BLK, N_DP, LOCAL)
    columns = jnp.arange(LOCAL, dtype=jnp.int32)

    def shard_step(carry, index):
        text_acc, loss_sum, coeff_sum, logit_sum = carry
        k = index // N_DP
        p = index % N_DP
        rows = x_half[k, p]
        first_sign = jnp.where(pairs[k, p][:, None] == columns[None, :], 1.0, -1.0).astype(jnp.float32)
        image_acc = jnp.zeros((LOCAL, D), jnp.float32)
        for step in range(STEPS):
            other = ((k - step) % N_BLK).astype(jnp.int32)
            cols = y_half[other, p]
            sign = first_sign if step == 0 else jnp.float32(-1.0)
            logits = scale * lax.dot_general(rows, cols, (((1,), (1,)), ((), ())), preferred_element_type=jnp.float32) + shift
            coeff = -sign * jax.nn.sigmoid(-sign * logits)
            loss_sum = loss_sum + jnp.sum(jax.nn.softplus(-sign * logits))
            coeff_sum = coeff_sum + jnp.sum(coeff)
            logit_sum = logit_sum + jnp.sum(coeff * (logits - shift))
            coeff_half = coeff.astype(jnp.bfloat16)
            image_acc = image_acc + jnp.dot(coeff_half, cols, preferred_element_type=jnp.float32)
            term = lax.dot_general(coeff_half, rows, (((0,), (0,)), ((), ())), preferred_element_type=jnp.float32)
            text_acc = text_acc.at[other, p].add(term)
        return ((text_acc, loss_sum, coeff_sum, logit_sum), image_acc)
    start = (jnp.zeros((N_BLK, N_DP, LOCAL, D), jnp.float32), jnp.float32(0.0), jnp.float32(0.0), jnp.float32(0.0))
    carry, image_accs = lax.scan(shard_step, start, jnp.arange(N_BLK * N_DP, dtype=jnp.int32))
    text_acc, loss_sum, coeff_sum, logit_sum = carry
    image_grad = backnorm(scale * image_accs.reshape(N_BLK, N_DP, LOCAL, D), x_full, x_factor)
    text_grad = backnorm(scale * text_acc, y_full, y_factor)
    count = jnp.float32(IMAGES)
    totals = jnp.stack([loss_sum, logit_sum, coeff_sum]) / count
    return (image_grad.reshape(IMAGES, D).astype(jnp.bfloat16), text_grad.reshape(IMAGES, D).astype(jnp.bfloat16), totals)
```

```python
import jax
import jax.numpy as jnp
from jax import lax
from jax.experimental import pallas as pl
from jax.experimental.pallas import tpu as pltpu
from jax.sharding import PartitionSpec as P

MESH = pl.DeviceIdType.MESH
BF16 = jnp.bfloat16
F32 = jnp.float32

ROWS = 512
WIDTH = 1152
COUNT = 131072.0
N_BLK = 32
PIECE = 64
PIECES = ROWS // PIECE
STEPS = 2 * PIECES
TILE = 128
HALF = 256
WINDOW = 3
PARTNER = STEPS * 2 * PIECE
SKIP = PARTNER + ROWS


def contract_last(a, b):
    return lax.dot_general(a, b, (((1,), (1,)), ((), ())), preferred_element_type=F32)


def contract_first(a, b):
    return lax.dot_general(a, b, (((0,), (0,)), ((), ())), preferred_element_type=F32)


def fold(v):
    return jnp.sum(v.reshape(v.shape[0] // 8, 8, v.shape[1]), axis=0)


def kernel(
    images, texts, positives, log_scale, bias,
    image_grad, text_grad, totals,
    raw, unit, factor, total, held, result, sums, share,
    load_sem, link_send, link_recv, pass_send, pass_recv, pair_send, pair_recv,
    skip_send, skip_recv, share_send, share_recv, out_sem,
):
    k = lax.axis_index("blk")
    p = lax.axis_index("dp")
    core = lax.rem(k, 2)
    pair = k + 1 - 2 * core
    skip = lax.rem(k - 3 + 6 * core + N_BLK, N_BLK)

    def load(side):
        return pltpu.make_async_copy((images, texts)[side], raw.at[side], load_sem.at[side])

    load(1).start()
    load(0).start()

    def group(level, i):
        if level == 0:
            digit = lax.rem(k, 4)
            return (k - digit + lax.rem(digit + i, 4), p)
        if level == 1:
            digit = lax.rem(k // 4, 4)
            return (k + 4 * (lax.rem(digit + i, 4) - digit), p)
        if level == 2:
            digit = lax.rem(p, 4)
            return (k, p - digit + lax.rem(digit + i, 4))
        digit = 2 * (k // 16) + p // 4
        other = lax.rem(digit + i, 4)
        return (lax.rem(k, 16) + 16 * (other // 2), lax.rem(p, 4) + 4 * lax.rem(other, 2))

    barrier = pltpu.get_barrier_semaphore()
    greeted = [(lax.rem(k + 2, N_BLK), p), (lax.rem(k - 2 + N_BLK, N_BLK), p), (pair, p), (skip, p)]
    greeted += [group(level, i) for level in range(4) for i in (1, 2, 3)]
    for device in greeted:
        pl.semaphore_signal(barrier, inc=1, device_id=device, device_id_type=MESH)

    def link(t):
        second = t // PIECES
        start = pl.multiple_of(PIECE * lax.rem(t, PIECES), PIECE)
        place = pl.multiple_of(2 * PIECE * t, PIECE)
        return pltpu.make_async_remote_copy(
            src_ref=unit.at[1 - second, pl.ds(start, PIECE)],
            dst_ref=held.at[pl.ds(place, PIECE)],
            send_sem=link_send.at[t],
            recv_sem=link_recv.at[t],
            device_id=(lax.rem(k + 2 - 4 * second + N_BLK, N_BLK), p),
            device_id_type=MESH,
        )

    def hand_on(t):
        place = pl.multiple_of(2 * PIECE * t, PIECE)
        return pltpu.make_async_remote_copy(
            src_ref=held.at[pl.ds(place, PIECE)],
            dst_ref=held.at[pl.ds(place + PIECE, PIECE)],
            send_sem=pass_send.at[t],
            recv_sem=pass_recv.at[t],
            device_id=(pair, p),
            device_id_type=MESH,
        )

    to_pair = pltpu.make_async_remote_copy(
        src_ref=unit.at[1 - core],
        dst_ref=held.at[pl.ds(PARTNER, ROWS)],
        send_sem=pair_send,
        recv_sem=pair_recv,
        device_id=(pair, p),
        device_id_type=MESH,
    )

    def to_skip(q):
        start = pl.multiple_of(TILE * q, TILE)
        return pltpu.make_async_remote_copy(
            src_ref=unit.at[core, pl.ds(start, TILE)],
            dst_ref=held.at[pl.ds(SKIP + start, TILE)],
            send_sem=skip_send.at[q],
            recv_sem=skip_recv.at[q],
            device_id=(skip, p),
            device_id_type=MESH,
        )

    def normalize(side, j):
        rows = pl.ds(pl.multiple_of(PIECE * j, PIECE), PIECE)
        full = raw[side, rows, :].astype(F32)
        scaler = lax.rsqrt(jnp.sum(full * full, axis=-1, keepdims=True) + 1e-06)
        unit[side, rows, :] = (full * scaler).astype(BF16)
        factor[side, rows, :] = jnp.broadcast_to(scaler, (PIECE, 128))

    load(1).wait()
    normalize(1, 0)
    pl.semaphore_wait(barrier, len(greeted))
    link(0).start()
    for j in range(1, WINDOW):
        normalize(1, j)
        link(j).start()

    @pl.loop(WINDOW, PIECES)
    def _(j):
        normalize(1, j)

    pl.when(core == 0)(to_pair.start)
    load(0).wait()

    @pl.loop(0, PIECES)
    def _(j):
        normalize(0, j)

    pl.when(core == 1)(to_pair.start)

    @pl.when(core == 0)
    def _():
        for q in range(4):
            to_skip(q).start()

    scale = jnp.exp(jnp.full((1, 128), log_scale[0], F32))
    shift = bias[0]
    sums[...] = jnp.zeros_like(sums)

    def count(weight, loss, logit, coeff):
        sums[0] += weight * fold(loss)
        sums[1] += weight * fold(logit)
        sums[2] += weight * fold(coeff)

    @pl.loop(0, ROWS // TILE)
    def _(c):
        cols = pl.ds(pl.multiple_of(TILE * c, TILE), TILE)
        rows = unit[0, cols, :]
        wanted = positives[:, cols]
        halves = []
        for h in range(2):
            part = pl.ds(HALF * h, HALF)
            product = scale * contract_last(unit[1, part, :], rows)
            logits = product + shift
            match = lax.broadcasted_iota(jnp.int32, (HALF, TILE), 0) + HALF * h == wanted
            odds = jnp.exp(jnp.where(match, -logits, logits))
            chance = odds / (1.0 + odds)
            coeff = jnp.where(match, -chance, chance)
            count(1.0, jnp.log1p(odds), coeff * product, coeff)
            coeff = coeff.astype(BF16)
            halves.append(coeff)
            term = jnp.dot(coeff, rows, preferred_element_type=F32)

            @pl.when(c == 0)
            def _():
                total[1, part, :] = term

            @pl.when(c > 0)
            def _():
                total[1, part, :] += term

        total[0, cols, :] = contract_first(jnp.concatenate(halves, axis=0), unit[1])

    def work(side, place, weight):
        other = held[pl.ds(pl.multiple_of(place, TILE), TILE), :]
        for h in range(2):
            part = pl.ds(HALF * h, HALF)
            product = scale * contract_last(unit[side, part, :], other)
            odds = jnp.exp(product + shift)
            coeff = odds / (1.0 + odds)
            if weight is not None:
                count(weight, jnp.log1p(odds), coeff * product, coeff)
            total[side, part, :] += jnp.dot(coeff.astype(BF16), other, preferred_element_type=F32)

    first_core = jnp.where(core == 0, 1.0, 0.0).astype(F32)
    second_core = 1.0 - first_core
    to_pair.wait_recv()

    @pl.loop(0, ROWS // TILE)
    def _(q):
        work(1 - core, PARTNER + TILE * q, first_core)

    lane = lax.broadcasted_iota(jnp.int32, (8, 128), 1)
    row = lax.broadcasted_iota(jnp.int32, (8, 128), 0)

    def exchange(level, i):
        return pltpu.make_async_remote_copy(
            src_ref=share.at[level, 0],
            dst_ref=share.at[level, i],
            send_sem=share_send.at[level, i - 1],
            recv_sem=share_recv.at[level, i - 1],
            device_id=group(level, i),
            device_id_type=MESH,
        )

    def gathered(level):
        for i in (1, 2, 3):
            exchange(level, i).wait_recv()
        return (share[level, 0] + share[level, 2]) + (share[level, 1] + share[level, 3])

    def send_share(level, value):
        share[level, 0] = value
        for i in (1, 2, 3):
            exchange(level, i).start()

    def step(t, weight):
        link(t).wait_recv()
        hand_on(t).start()
        hand_on(t).wait_recv()
        work(t // PIECES, 2 * PIECE * t, weight)

    @pl.loop(0, STEPS - 1)
    def _(t):
        link(t).wait_send()

        @pl.when(t + WINDOW < STEPS)
        def _():
            link(t + WINDOW).start()

        @pl.when((t == PIECES) & (core == 1))
        def _():
            for q in range(4):
                to_skip(q).start()

        @pl.when(t == PIECES)
        def _():
            value = jnp.zeros((8, 128), F32)
            for i in range(3):
                value = jnp.where(lane == i, jnp.sum(sums[i]), value)
            send_share(0, value)

        for level in range(3):
            @pl.when(t == PIECES + 1 + level)
            def _():
                send_share(level + 1, gathered(level))

        step(t, jnp.where(t < PIECES, 1.0, 0.0).astype(F32))
        at = lax.rem(t, PIECES)

        @pl.when((t // PIECES == 1 - core) & (at >= 2) & (at < 6))
        def _():
            to_skip(at - 2).wait_recv()
            work(core, SKIP + TILE * (at - 2), second_core)

    def finish(side, j):
        rows = pl.ds(pl.multiple_of(PIECE * j, PIECE), PIECE)
        full = raw[side, rows, :].astype(F32)
        grad = total[side, rows, :]
        scaler = factor[side, rows, 0:1]
        inner = scaler * scaler * jnp.sum(full * grad, axis=-1, keepdims=True)
        result[side, rows, :] = (scale[:, 0:1] * scaler * (grad - full * inner)).astype(BF16)
        return pltpu.make_async_copy(
            result.at[side, rows], (image_grad, text_grad)[side].at[rows], out_sem.at[side, j]
        )

    @pl.loop(0, PIECES)
    def _(j):
        finish(0, j).start()

    answer = gathered(3)
    for i in range(3):
        picked = jnp.sum(jnp.where((lane == i) & (row == 0), answer, 0.0))
        totals[i] = picked / COUNT

    link(STEPS - 1).wait_send()
    step(STEPS - 1, None)

    @pl.loop(0, PIECES)
    def _(j):
        finish(1, j).start()

    to_pair.wait_send()
    for q in range(4):
        to_skip(q).wait_send()
    for level in range(4):
        for i in (1, 2, 3):
            exchange(level, i).wait_send()

    @pl.loop(0, STEPS)
    def _(t):
        hand_on(t).wait_send()

    @pl.loop(0, PIECES)
    def _(j):
        rows = pl.ds(pl.multiple_of(PIECE * j, PIECE), PIECE)
        for side in range(2):
            pltpu.make_async_copy(
                result.at[side, rows], (image_grad, text_grad)[side].at[rows], out_sem.at[side, j]
            ).wait()


def body(images, texts, positives, log_scale, bias):
    anywhere = pl.BlockSpec(memory_space=pl.ANY)
    smem = pl.BlockSpec(memory_space=pltpu.SMEM)
    dma = pltpu.SemaphoreType.DMA
    return pl.pallas_call(
        kernel,
        out_shape=(
            jax.ShapeDtypeStruct((ROWS, WIDTH), BF16),
            jax.ShapeDtypeStruct((ROWS, WIDTH), BF16),
            jax.ShapeDtypeStruct((3,), F32),
        ),
        in_specs=[anywhere, anywhere, pl.BlockSpec(memory_space=pltpu.VMEM), smem, smem],
        out_specs=(anywhere, anywhere, smem),
        scratch_shapes=[
            pltpu.VMEM((2, ROWS, WIDTH), BF16),
            pltpu.VMEM((2, ROWS, WIDTH), BF16),
            pltpu.VMEM((2, ROWS, 128), F32),
            pltpu.VMEM((2, ROWS, WIDTH), F32),
            pltpu.VMEM((SKIP + ROWS, WIDTH), BF16),
            pltpu.VMEM((2, ROWS, WIDTH), BF16),
            pltpu.VMEM((3, 8, 128), F32),
            pltpu.VMEM((4, 4, 8, 128), F32),
            dma((2,)),
            dma((STEPS,)),
            dma((STEPS,)),
            dma((STEPS,)),
            dma((STEPS,)),
            dma,
            dma,
            dma((4,)),
            dma((4,)),
            dma((4, 3)),
            dma((4, 3)),
            dma((2, PIECES)),
        ],
        compiler_params=pltpu.CompilerParams(
            collective_id=0, has_side_effects=True, vmem_limit_bytes=48 << 20
        ),
        cost_estimate=pl.CostEstimate(
            flops=15 * 2 * ROWS * ROWS * WIDTH, bytes_accessed=4 * ROWS * WIDTH * 2, transcendentals=0
        ),
    )(images, texts, positives, log_scale, bias)


def solution(mesh):
    return jax.shard_map(
        body,
        mesh=mesh,
        in_specs=(P(("blk", "dp"), None), P(("blk", "dp"), None), P(("blk", "dp"), None), P(), P()),
        out_specs=(P(("blk", "dp"), None), P(("blk", "dp"), None), P()),
        check_vma=False,
    )
```

```python
import jax
import jax.numpy as jnp
from jax import lax
from jax.experimental import pallas as pl
from jax.experimental.pallas import tpu as pltpu
from jax.sharding import PartitionSpec as P

MESH = pl.DeviceIdType.MESH
BF16 = jnp.bfloat16
F32 = jnp.float32

ROWS = 512
WIDTH = 1152
COUNT = 131072.0
N_BLK = 32
N_DP = 8
PIECE = 64
PIECES = ROWS // PIECE
STEPS = 2 * PIECES
TILE = 128
HALF = 256
PARTNER = STEPS * 2 * PIECE
SKIP = PARTNER + ROWS


LEVELS = 4


def others(level):
    return range(1, 2) if level < 2 else range(1, 8)


def contract_last(a, b):
    return lax.dot_general(a, b, (((1,), (1,)), ((), ())), preferred_element_type=F32)


def contract_first(a, b):
    return lax.dot_general(a, b, (((0,), (0,)), ((), ())), preferred_element_type=F32)


def fold(v):
    return jnp.sum(v.reshape(v.shape[0] // 8, 8, v.shape[1]), axis=0)


def kernel(
    images, texts, positives, log_scale, bias,
    image_grad, text_grad, answer,
    raw, unit, factor, total, held, result, sums, share,
    load_sem, link_send, link_recv, pass_send, pass_recv, pair_send, pair_recv,
    skip_send, skip_recv, share_send, share_recv, out_sem,
):
    k = lax.axis_index("blk")
    p = lax.axis_index("dp")
    core = lax.rem(k, 2)
    odd = lax.rem(k // 2, 2)
    pair = k + 1 - 2 * core
    skip = lax.rem(k - 3 + 6 * core + N_BLK, N_BLK)

    def load(side):
        return pltpu.make_async_copy((images, texts)[side], raw.at[side], load_sem.at[side])

    load(1).start()
    load(0).start()

    def group(level, i):
        if level == 0:
            return (pair, p)
        if level == 1:
            return (k + 3 - 2 * lax.rem(k, 4), p)
        if level == 2:
            return (lax.rem(k + 4 * i, N_BLK), p)
        return (k, lax.rem(p + i, N_DP))

    barrier = pltpu.get_barrier_semaphore()
    greeted = [(lax.rem(k + 2, N_BLK), p), (lax.rem(k - 2 + N_BLK, N_BLK), p), (pair, p), (skip, p)]
    greeted += [group(level, i) for level in range(1, LEVELS) for i in others(level)]
    for device in greeted:
        pl.semaphore_signal(barrier, inc=1, device_id=device, device_id_type=MESH)

    def link(t):
        second = t // PIECES
        start = pl.multiple_of(PIECE * lax.rem(t, PIECES), PIECE)
        place = pl.multiple_of(2 * PIECE * t, PIECE)
        return pltpu.make_async_remote_copy(
            src_ref=unit.at[1 - second, pl.ds(start, PIECE)],
            dst_ref=held.at[pl.ds(place, PIECE)],
            send_sem=link_send.at[t],
            recv_sem=link_recv.at[t],
            device_id=(lax.rem(k + 2 - 4 * second + N_BLK, N_BLK), p),
            device_id_type=MESH,
        )

    def hand_on(t):
        place = pl.multiple_of(2 * PIECE * t, PIECE)
        return pltpu.make_async_remote_copy(
            src_ref=held.at[pl.ds(place, PIECE)],
            dst_ref=held.at[pl.ds(place + PIECE, PIECE)],
            send_sem=pass_send.at[t],
            recv_sem=pass_recv.at[t],
            device_id=(pair, p),
            device_id_type=MESH,
        )

    to_pair = pltpu.make_async_remote_copy(
        src_ref=unit.at[1 - core],
        dst_ref=held.at[pl.ds(PARTNER, ROWS)],
        send_sem=pair_send,
        recv_sem=pair_recv,
        device_id=(pair, p),
        device_id_type=MESH,
    )

    def to_skip(q):
        start = pl.multiple_of(TILE * q, TILE)
        return pltpu.make_async_remote_copy(
            src_ref=unit.at[core, pl.ds(start, TILE)],
            dst_ref=held.at[pl.ds(SKIP + start, TILE)],
            send_sem=skip_send.at[q],
            recv_sem=skip_recv.at[q],
            device_id=(skip, p),
            device_id_type=MESH,
        )

    def normalize(side, j):
        rows = pl.ds(pl.multiple_of(PIECE * j, PIECE), PIECE)
        full = raw[side, rows, :].astype(F32)
        scaler = lax.rsqrt(jnp.sum(full * full, axis=-1, keepdims=True) + 1e-06)
        unit[side, rows, :] = (full * scaler).astype(BF16)
        factor[side, rows, :] = jnp.broadcast_to(scaler, (PIECE, 128))

    load(1).wait()
    normalize(1, 0)
    pl.semaphore_wait(barrier, len(greeted))
    link(0).start()

    @pl.loop(1, PIECES)
    def _(j):
        normalize(1, j)
        link(j).start()

    pl.when(core == 0)(to_pair.start)
    load(0).wait()

    @pl.loop(0, PIECES)
    def _(j):
        normalize(0, j)

    pl.when(core == 1)(to_pair.start)

    def send_skip():
        for q in range(4):
            to_skip(q).start()

    pl.when(odd * core == 0)(send_skip)

    @pl.when(odd == 1)
    def _():
        @pl.loop(PIECES, STEPS)
        def _(t):
            link(t).start()

    scale = jnp.exp(jnp.full((1, 128), log_scale[0], F32))
    shift = bias[0]
    sums[...] = jnp.zeros_like(sums)

    def count(weight, loss, logit, coeff):
        sums[0] += weight * fold(loss)
        sums[1] += weight * fold(logit)
        sums[2] += weight * fold(coeff)

    @pl.loop(0, ROWS // TILE)
    def _(c):
        cols = pl.ds(pl.multiple_of(TILE * c, TILE), TILE)
        rows = unit[0, cols, :]
        wanted = positives[:, cols]
        halves = []
        for h in range(2):
            part = pl.ds(HALF * h, HALF)
            product = scale * contract_last(unit[1, part, :], rows)
            logits = product + shift
            match = lax.broadcasted_iota(jnp.int32, (HALF, TILE), 0) + HALF * h == wanted
            odds = jnp.exp(jnp.where(match, -logits, logits))
            chance = odds / (1.0 + odds)
            coeff = jnp.where(match, -chance, chance)
            count(1.0, jnp.log1p(odds), coeff * product, coeff)
            coeff = coeff.astype(BF16)
            halves.append(coeff)
            term = jnp.dot(coeff, rows, preferred_element_type=F32)

            @pl.when(c == 0)
            def _():
                total[1, part, :] = term

            @pl.when(c > 0)
            def _():
                total[1, part, :] += term

        total[0, cols, :] = contract_first(jnp.concatenate(halves, axis=0), unit[1])

    def work(side, place, weight):
        other = held[pl.ds(pl.multiple_of(place, TILE), TILE), :]
        for h in range(2):
            part = pl.ds(HALF * h, HALF)
            product = scale * contract_last(unit[side, part, :], other)
            odds = jnp.exp(product + shift)
            coeff = odds / (1.0 + odds)
            if weight is not None:
                count(weight, jnp.log1p(odds), coeff * product, coeff)
            total[side, part, :] += jnp.dot(coeff.astype(BF16), other, preferred_element_type=F32)

    first_core = jnp.where(core == 0, 1.0, 0.0).astype(F32)
    second_core = 1.0 - first_core
    to_pair.wait_recv()

    @pl.loop(0, ROWS // TILE)
    def _(q):
        work(1 - core, PARTNER + TILE * q, first_core)

    lane = lax.broadcasted_iota(jnp.int32, (8, 128), 1)

    def exchange(level, i):
        return pltpu.make_async_remote_copy(
            src_ref=share.at[level, 0],
            dst_ref=share.at[level, i],
            send_sem=share_send.at[level, i - 1],
            recv_sem=share_recv.at[level, i - 1],
            device_id=group(level, i),
            device_id_type=MESH,
        )

    def gathered(level):
        for i in others(level):
            exchange(level, i).wait_recv()
        parts = [share[level, i] for i in range(len(others(level)) + 1)]
        while len(parts) > 1:
            half = len(parts) // 2
            parts = [parts[i] + parts[i + half] for i in range(half)]
        return parts[0]

    def send_share(level, value):
        share[level, 0] = value
        for i in others(level):
            exchange(level, i).start()

    def arrive(t):
        link(t).wait_recv()
        hand_on(t).start()

    def use(t, weight):
        hand_on(t).wait_recv()
        work(t // PIECES, 2 * PIECE * t, weight)

    def order(s):
        middle = lax.rem((s // 4 + 1) // 2, 2)
        piece = (s + 4) // 2 + 4 * lax.rem(s + 1, 2)
        return s + odd * middle * (piece - s)

    @pl.loop(0, 13)
    def _(s):
        arrive(order(s))

        @pl.when((odd == 0) & (s >= 2) & (s <= 8) & (lax.rem(s, 2) == 0))
        def _():
            link(PIECES - 1 + s // 2).start()

        @pl.when((odd == 0) & (s >= 10))
        def _():
            link(PIECES - 6 + s).start()

        pl.when((odd * core == 1) & (s == 7))(send_skip)

        @pl.when(s > 0)
        def _():
            t = order(s - 1)
            use(t, 1.0 - (t // PIECES).astype(F32))

        @pl.when(s >= 9)
        def _():
            to_skip(s - 9).wait_recv()
            work(core, SKIP + TILE * (s - 9), second_core)

    value = jnp.zeros((8, 128), F32)
    for i in range(3):
        value = jnp.where(lane == i, jnp.sum(sums[i]), value)
    send_share(0, value)
    use(12, None)
    arrive(13)

    @pl.when(odd == 0)
    def _():
        link(STEPS - 1).start()

    send_share(1, gathered(0))
    use(13, None)

    def leave(side, j):
        rows = pl.ds(pl.multiple_of(PIECE * j, PIECE), PIECE)
        return pltpu.make_async_copy(
            result.at[side, rows], (image_grad, text_grad)[side].at[rows], out_sem.at[side, j]
        )

    def finish(side, j):
        rows = pl.ds(pl.multiple_of(PIECE * j, PIECE), PIECE)
        full = raw[side, rows, :].astype(F32)
        grad = total[side, rows, :]
        scaler = factor[side, rows, 0:1]
        inner = scaler * scaler * jnp.sum(full * grad, axis=-1, keepdims=True)
        result[side, rows, :] = (scale[:, 0:1] * scaler * (grad - full * inner)).astype(BF16)
        leave(side, j).start()

    arrive(14)
    send_share(2, gathered(1))

    @pl.loop(0, PIECES)
    def _(j):
        finish(0, j)

    use(14, None)
    arrive(15)
    send_share(3, gathered(2))
    use(15, None)

    @pl.loop(0, PIECES)
    def _(j):
        finish(1, j)

    found = gathered(3)
    for i in range(3):
        answer[i] = jnp.max(jnp.where(lane == i, found, -jnp.inf)) / COUNT
    to_pair.wait_send()
    for q in range(4):
        to_skip(q).wait_send()
    for level in range(LEVELS):
        for i in others(level):
            exchange(level, i).wait_send()

    @pl.loop(0, STEPS)
    def _(t):
        link(t).wait_send()
        hand_on(t).wait_send()

    @pl.loop(0, PIECES)
    def _(j):
        leave(0, j).wait()
        leave(1, j).wait()


def write(image, text, answer, image_grad, text_grad, totals, rows_held, totals_held, load_sem, store_sem):
    loads = [pltpu.make_async_copy(answer, totals_held, load_sem.at[2, 0])]
    stores = [pltpu.make_async_copy(totals_held, totals, store_sem.at[2, 0])]
    for i, (source, target) in enumerate(((image, image_grad), (text, text_grad))):
        for j in range(4):
            rows = pl.ds(TILE * j, TILE)
            loads.append(pltpu.make_async_copy(source.at[rows], rows_held.at[i, rows], load_sem.at[i, j]))
            stores.append(pltpu.make_async_copy(rows_held.at[i, rows], target.at[rows], store_sem.at[i, j]))
    for load in loads:
        load.start()
    for load, store in zip(loads, stores):
        load.wait()
        store.start()
    for store in stores:
        store.wait()


def body(images, texts, positives, log_scale, bias):
    hbm = pl.BlockSpec(memory_space=pltpu.HBM)
    vmem = pl.BlockSpec(memory_space=pltpu.VMEM)
    smem = pl.BlockSpec(memory_space=pltpu.SMEM)
    dma = pltpu.SemaphoreType.DMA
    grad = jax.ShapeDtypeStruct((ROWS, WIDTH), BF16)
    three = jax.ShapeDtypeStruct((3,), F32)
    image, text, answer = pl.pallas_call(
        kernel,
        out_shape=(grad, grad, three),
        in_specs=[hbm, hbm, vmem, smem, smem],
        out_specs=(hbm, hbm, smem),
        scratch_shapes=[
            pltpu.VMEM((2, ROWS, WIDTH), BF16),
            pltpu.VMEM((2, ROWS, WIDTH), BF16),
            pltpu.VMEM((2, ROWS, 128), F32),
            pltpu.VMEM((2, ROWS, WIDTH), F32),
            pltpu.VMEM((SKIP + ROWS, WIDTH), BF16),
            pltpu.VMEM((2, ROWS, WIDTH), BF16),
            pltpu.VMEM((3, 8, 128), F32),
            pltpu.VMEM((LEVELS, 8, 8, 128), F32),
            dma((2,)),
            dma((STEPS,)),
            dma((STEPS,)),
            dma((STEPS,)),
            dma((STEPS,)),
            dma,
            dma,
            dma((4,)),
            dma((4,)),
            dma((LEVELS, 7)),
            dma((LEVELS, 7)),
            dma((2, PIECES)),
        ],
        compiler_params=pltpu.CompilerParams(
            collective_id=0, has_side_effects=True, vmem_limit_bytes=58 << 20
        ),
        cost_estimate=pl.CostEstimate(
            flops=15 * 2 * ROWS * ROWS * WIDTH, bytes_accessed=4 * ROWS * WIDTH * 2, transcendentals=0
        ),
    )(images, texts, positives, log_scale, bias)
    return pl.pallas_call(
        write,
        out_shape=(grad, grad, three),
        in_specs=[hbm, hbm, hbm],
        out_specs=(hbm, hbm, hbm),
        scratch_shapes=[
            pltpu.VMEM((2, ROWS, WIDTH), BF16),
            pltpu.SMEM((3,), F32),
            dma((3, 4)),
            dma((3, 4)),
        ],
        compiler_params=pltpu.CompilerParams(vmem_limit_bytes=60 << 20),
    )(image, text, answer)


def solution(mesh):
    return jax.shard_map(
        body,
        mesh=mesh,
        in_specs=(P(("blk", "dp"), None), P(("blk", "dp"), None), P(("blk", "dp"), None), P(), P()),
        out_specs=(P(("blk", "dp"), None), P(("blk", "dp"), None), P()),
        check_vma=False,
    )
```

```python
import jax
import jax.numpy as jnp
from jax import lax
from jax.experimental import pallas as pl
from jax.experimental.pallas import tpu as pltpu
from jax.sharding import PartitionSpec as P

MESH = pl.DeviceIdType.MESH
BF16 = jnp.bfloat16
F32 = jnp.float32

ROWS = 512
WIDTH = 1152
COUNT = 131072.0
N_BLK = 32
N_DP = 8
PIECE = 64
PIECES = ROWS // PIECE
STEPS = 2 * PIECES
TILE = 128
HALF = 256
PARTNER = STEPS * 2 * PIECE
SKIP = PARTNER + ROWS


LEVELS = 6
MIDDLE = (2, 3, 4)


def others(level):
    return range(1, (2, 2, 2, 8, 4, 2)[level])


def contract_last(a, b):
    return lax.dot_general(a, b, (((1,), (1,)), ((), ())), preferred_element_type=F32)


def contract_first(a, b):
    return lax.dot_general(a, b, (((0,), (0,)), ((), ())), preferred_element_type=F32)


def fold(v):
    return jnp.sum(v.reshape(v.shape[0] // 8, 8, v.shape[1]), axis=0)


def kernel(
    images, texts, positives, log_scale, bias,
    image_grad, text_grad, answer,
    raw, unit, factor, total, held, result, sums, share,
    load_sem, link_send, link_recv, pass_send, pass_recv, pair_send, pair_recv,
    skip_send, skip_recv, share_send, share_recv, out_sem, go_sem,
):
    k = lax.axis_index("blk")
    p = lax.axis_index("dp")
    core = lax.rem(k, 2)
    odd = lax.rem(k // 2, 2)
    pair = k + 1 - 2 * core
    skip = lax.rem(k - 3 + 6 * core + N_BLK, N_BLK)

    def load(side):
        return pltpu.make_async_copy((images, texts)[side], raw.at[side], load_sem.at[side])

    load(1).start()
    load(0).start()

    def group(level, i):
        if level == 0:
            return (pair, p)
        if level == 1 or level == 5:
            return (lax.rem(k + 6 - 12 * odd + N_BLK, N_BLK), p)
        if level == 2:
            return (lax.rem(k + N_BLK // 2, N_BLK), p + 1 - 2 * lax.rem(p, 2))
        if level == 3:
            return (lax.rem(k + 4 * i, N_BLK), p)
        return (k, lax.rem(p + 2 * i, N_DP))

    barrier = pltpu.get_barrier_semaphore()
    greeted = [(lax.rem(k + 2, N_BLK), p), (lax.rem(k - 2 + N_BLK, N_BLK), p), (pair, p), (skip, p), group(1, 1)]
    for device in greeted:
        pl.semaphore_signal(barrier, inc=1, device_id=device, device_id_type=MESH)

    @pl.when(odd == 1)
    def _():
        for level in MIDDLE:
            for i in others(level):
                pl.semaphore_signal(barrier, inc=1, device_id=group(level, i), device_id_type=MESH)

    greetings = len(greeted) + odd * sum(len(others(level)) for level in MIDDLE)

    def link(t):
        second = t // PIECES
        start = pl.multiple_of(PIECE * lax.rem(t, PIECES), PIECE)
        place = pl.multiple_of(2 * PIECE * t, PIECE)
        return pltpu.make_async_remote_copy(
            src_ref=unit.at[1 - second, pl.ds(start, PIECE)],
            dst_ref=held.at[pl.ds(place, PIECE)],
            send_sem=link_send.at[t],
            recv_sem=link_recv.at[t],
            device_id=(lax.rem(k + 2 - 4 * second + N_BLK, N_BLK), p),
            device_id_type=MESH,
        )

    def hand_on(t):
        place = pl.multiple_of(2 * PIECE * t, PIECE)
        return pltpu.make_async_remote_copy(
            src_ref=held.at[pl.ds(place, PIECE)],
            dst_ref=held.at[pl.ds(place + PIECE, PIECE)],
            send_sem=pass_send.at[t],
            recv_sem=pass_recv.at[t],
            device_id=(pair, p),
            device_id_type=MESH,
        )

    to_pair = pltpu.make_async_remote_copy(
        src_ref=unit.at[1 - core],
        dst_ref=held.at[pl.ds(PARTNER, ROWS)],
        send_sem=pair_send,
        recv_sem=pair_recv,
        device_id=(pair, p),
        device_id_type=MESH,
    )

    def to_skip(q):
        start = pl.multiple_of(TILE * q, TILE)
        return pltpu.make_async_remote_copy(
            src_ref=unit.at[core, pl.ds(start, TILE)],
            dst_ref=held.at[pl.ds(SKIP + start, TILE)],
            send_sem=skip_send.at[q],
            recv_sem=skip_recv.at[q],
            device_id=(skip, p),
            device_id_type=MESH,
        )

    def normalize(side, j):
        rows = pl.ds(pl.multiple_of(PIECE * j, PIECE), PIECE)
        full = raw[side, rows, :].astype(F32)
        scaler = lax.rsqrt(jnp.sum(full * full, axis=-1, keepdims=True) + 1e-06)
        unit[side, rows, :] = (full * scaler).astype(BF16)
        factor[side, rows, :] = jnp.broadcast_to(scaler, (PIECE, 128))

    load(1).wait()
    normalize(1, 0)
    pl.semaphore_wait(barrier, greetings)
    link(0).start()

    @pl.loop(1, PIECES)
    def _(j):
        normalize(1, j)
        link(j).start()

    pl.when(core == 0)(to_pair.start)
    load(0).wait()

    @pl.loop(0, PIECES)
    def _(j):
        normalize(0, j)

    pl.when(core == 1)(to_pair.start)

    def send_skip():
        for q in range(4):
            to_skip(q).start()

    pl.when(odd * core == 0)(send_skip)

    @pl.when(odd == 1)
    def _():
        @pl.loop(PIECES, STEPS)
        def _(t):
            link(t).start()

    scale = jnp.exp(jnp.full((1, 128), log_scale[0], F32))
    shift = bias[0]
    sums[...] = jnp.zeros_like(sums)

    def count(weight, loss, logit, coeff):
        sums[0] += weight * fold(loss)
        sums[1] += weight * fold(logit)
        sums[2] += weight * fold(coeff)

    @pl.loop(0, ROWS // TILE)
    def _(c):
        cols = pl.ds(pl.multiple_of(TILE * c, TILE), TILE)
        rows = unit[0, cols, :]
        wanted = positives[:, cols]
        halves = []
        for h in range(2):
            part = pl.ds(HALF * h, HALF)
            product = scale * contract_last(unit[1, part, :], rows)
            logits = product + shift
            match = lax.broadcasted_iota(jnp.int32, (HALF, TILE), 0) + HALF * h == wanted
            odds = jnp.exp(jnp.where(match, -logits, logits))
            chance = odds / (1.0 + odds)
            coeff = jnp.where(match, -chance, chance)
            count(1.0, jnp.log1p(odds), coeff * product, coeff)
            coeff = coeff.astype(BF16)
            halves.append(coeff)
            term = jnp.dot(coeff, rows, preferred_element_type=F32)

            @pl.when(c == 0)
            def _():
                total[1, part, :] = term

            @pl.when(c > 0)
            def _():
                total[1, part, :] += term

        total[0, cols, :] = contract_first(jnp.concatenate(halves, axis=0), unit[1])

    def work(side, place, weight):
        other = held[pl.ds(pl.multiple_of(place, TILE), TILE), :]
        for h in range(2):
            part = pl.ds(HALF * h, HALF)
            product = scale * contract_last(unit[side, part, :], other)
            odds = jnp.exp(product + shift)
            coeff = odds / (1.0 + odds)
            if weight is not None:
                count(weight, jnp.log1p(odds), coeff * product, coeff)
            total[side, part, :] += jnp.dot(coeff.astype(BF16), other, preferred_element_type=F32)

    first_core = jnp.where(core == 0, 1.0, 0.0).astype(F32)
    second_core = 1.0 - first_core
    to_pair.wait_recv()

    @pl.loop(0, ROWS // TILE)
    def _(q):
        work(1 - core, PARTNER + TILE * q, first_core)

    lane = lax.broadcasted_iota(jnp.int32, (8, 128), 1)

    def exchange(level, i):
        return pltpu.make_async_remote_copy(
            src_ref=share.at[level, 0],
            dst_ref=share.at[level, i],
            send_sem=share_send.at[level, i - 1],
            recv_sem=share_recv.at[level, i - 1],
            device_id=group(level, i),
            device_id_type=MESH,
        )

    def gathered(level):
        for i in others(level):
            exchange(level, i).wait_recv()
        parts = [share[level, i] for i in range(len(others(level)) + 1)]
        while len(parts) > 1:
            half = len(parts) // 2
            parts = [parts[i] + parts[i + half] for i in range(half)]
        return parts[0]

    def send_share(level, value):
        share[level, 0] = value
        for i in others(level):
            exchange(level, i).start()

    def arrive(t):
        link(t).wait_recv()
        hand_on(t).start()

    def use(t, weight):
        hand_on(t).wait_recv()
        work(t // PIECES, 2 * PIECE * t, weight)

    ahead = (lax.rem(k + 2, N_BLK), p)

    @pl.loop(0, STEPS - 2)
    def _(t):
        arrive(t)

        @pl.when((odd == 0) & (t == PIECES - 1))
        def _():
            pl.semaphore_wait(go_sem, 1)

            @pl.loop(PIECES, STEPS)
            def _(i):
                link(i).start()

        pl.when((odd * core == 1) & (t == PIECES - 1))(send_skip)

        @pl.when(t > 0)
        def _():
            use(t - 1, jnp.where(t <= PIECES, 1.0, 0.0).astype(F32))

        @pl.when((odd == 1) & (t == PIECES - 2))
        def _():
            pl.semaphore_signal(go_sem, inc=1, device_id=ahead, device_id_type=MESH)

        q = t - 9 + 5 * core

        @pl.when((q >= 0) & (q < 4))
        def _():
            to_skip(q).wait_recv()
            work(core, SKIP + TILE * q, second_core)

        @pl.when(t == PIECES)
        def _():
            value = jnp.zeros((8, 128), F32)
            for i in range(3):
                value = jnp.where(lane == i, jnp.sum(sums[i]), value)
            send_share(0, value)

        @pl.when((odd == 0) & (t == PIECES + 1))
        def _():
            send_share(1, gathered(0))

        @pl.when((odd == 1) & (t == PIECES + 1))
        def _():
            share[1, 0] = gathered(0)

        for level in MIDDLE:
            @pl.when((odd == 1) & (t == PIECES + level))
            def _():
                send_share(level, gathered(level - 1))

        @pl.when((odd == 1) & (t == PIECES + 5))
        def _():
            send_share(5, gathered(4))

    def leave(side, j):
        rows = pl.ds(pl.multiple_of(PIECE * j, PIECE), PIECE)
        return pltpu.make_async_copy(
            result.at[side, rows], (image_grad, text_grad)[side].at[rows], out_sem.at[side, j]
        )

    def finish(side, j):
        rows = pl.ds(pl.multiple_of(PIECE * j, PIECE), PIECE)
        full = raw[side, rows, :].astype(F32)
        grad = total[side, rows, :]
        scaler = factor[side, rows, 0:1]
        inner = scaler * scaler * jnp.sum(full * grad, axis=-1, keepdims=True)
        result[side, rows, :] = (scale[:, 0:1] * scaler * (grad - full * inner)).astype(BF16)
        leave(side, j).start()

    arrive(STEPS - 2)
    use(STEPS - 3, None)

    @pl.loop(0, PIECES)
    def _(j):
        finish(0, j)

    use(STEPS - 2, None)

    @pl.when(odd == 0)
    def _():
        exchange(5, 1).wait_recv()
        share[5, 0] = share[5, 1]

    found = share[5, 0]
    for i in range(3):
        answer[i] = jnp.max(jnp.where(lane == i, found, -jnp.inf)) / COUNT
    arrive(STEPS - 1)
    use(STEPS - 1, None)

    @pl.loop(0, PIECES)
    def _(j):
        finish(1, j)

    to_pair.wait_send()
    for q in range(4):
        to_skip(q).wait_send()
    exchange(0, 1).wait_send()
    pl.when(odd == 0)(exchange(1, 1).wait_send)

    @pl.when(odd == 1)
    def _():
        for level in (*MIDDLE, 5):
            for i in others(level):
                exchange(level, i).wait_send()

    @pl.loop(0, STEPS)
    def _(t):
        link(t).wait_send()
        hand_on(t).wait_send()

    @pl.loop(0, PIECES)
    def _(j):
        leave(0, j).wait()
        leave(1, j).wait()


def write(image, text, answer, image_grad, text_grad, totals, rows_held, totals_held, load_sem, store_sem):
    loads = [pltpu.make_async_copy(answer, totals_held, load_sem.at[2, 0])]
    stores = [pltpu.make_async_copy(totals_held, totals, store_sem.at[2, 0])]
    for i, (source, target) in enumerate(((image, image_grad), (text, text_grad))):
        for j in range(4):
            rows = pl.ds(TILE * j, TILE)
            loads.append(pltpu.make_async_copy(source.at[rows], rows_held.at[i, rows], load_sem.at[i, j]))
            stores.append(pltpu.make_async_copy(rows_held.at[i, rows], target.at[rows], store_sem.at[i, j]))
    for load in loads:
        load.start()
    for load, store in zip(loads, stores):
        load.wait()
        store.start()
    for store in stores:
        store.wait()


def body(images, texts, positives, log_scale, bias):
    hbm = pl.BlockSpec(memory_space=pltpu.HBM)
    vmem = pl.BlockSpec(memory_space=pltpu.VMEM)
    smem = pl.BlockSpec(memory_space=pltpu.SMEM)
    dma = pltpu.SemaphoreType.DMA
    grad = jax.ShapeDtypeStruct((ROWS, WIDTH), BF16)
    three = jax.ShapeDtypeStruct((3,), F32)
    image, text, answer = pl.pallas_call(
        kernel,
        out_shape=(grad, grad, three),
        in_specs=[hbm, hbm, vmem, smem, smem],
        out_specs=(hbm, hbm, smem),
        scratch_shapes=[
            pltpu.VMEM((2, ROWS, WIDTH), BF16),
            pltpu.VMEM((2, ROWS, WIDTH), BF16),
            pltpu.VMEM((2, ROWS, 128), F32),
            pltpu.VMEM((2, ROWS, WIDTH), F32),
            pltpu.VMEM((SKIP + ROWS, WIDTH), BF16),
            pltpu.VMEM((2, ROWS, WIDTH), BF16),
            pltpu.VMEM((3, 8, 128), F32),
            pltpu.VMEM((LEVELS, 8, 8, 128), F32),
            dma((2,)),
            dma((STEPS,)),
            dma((STEPS,)),
            dma((STEPS,)),
            dma((STEPS,)),
            dma,
            dma,
            dma((4,)),
            dma((4,)),
            dma((LEVELS, 7)),
            dma((LEVELS, 7)),
            dma((2, PIECES)),
            pltpu.SemaphoreType.REGULAR,
        ],
        compiler_params=pltpu.CompilerParams(
            collective_id=0, has_side_effects=True, vmem_limit_bytes=58 << 20
        ),
        cost_estimate=pl.CostEstimate(
            flops=15 * 2 * ROWS * ROWS * WIDTH, bytes_accessed=4 * ROWS * WIDTH * 2, transcendentals=0
        ),
    )(images, texts, positives, log_scale, bias)
    return pl.pallas_call(
        write,
        out_shape=(grad, grad, three),
        in_specs=[hbm, hbm, hbm],
        out_specs=(hbm, hbm, hbm),
        scratch_shapes=[
            pltpu.VMEM((2, ROWS, WIDTH), BF16),
            pltpu.SMEM((3,), F32),
            dma((3, 4)),
            dma((3, 4)),
        ],
        compiler_params=pltpu.CompilerParams(vmem_limit_bytes=60 << 20),
    )(image, text, answer)


def solution(mesh):
    return jax.shard_map(
        body,
        mesh=mesh,
        in_specs=(P(("blk", "dp"), None), P(("blk", "dp"), None), P(("blk", "dp"), None), P(), P()),
        out_specs=(P(("blk", "dp"), None), P(("blk", "dp"), None), P()),
        check_vma=False,
    )
```

```python
import jax
import jax.numpy as jnp
from jax import lax
from jax.experimental import pallas as pl
from jax.experimental.pallas import tpu as pltpu
from jax.sharding import PartitionSpec as P

MESH = pl.DeviceIdType.MESH
BF16 = jnp.bfloat16
F32 = jnp.float32

ROWS = 512
WIDTH = 1152
COUNT = 131072.0
N_BLK = 32
N_DP = 8
PIECE = 64
PIECES = ROWS // PIECE
STEPS = 2 * PIECES
TILE = 128
HALF = 256
PARTNER = STEPS * 2 * PIECE
SKIP = PARTNER + ROWS


LEVELS = 7
MIDDLE = (2, 3, 4)


def others(level):
    return range(1, (2, 2, 2, 8, 4, 2, 2)[level])


def contract_last(a, b):
    return lax.dot_general(a, b, (((1,), (1,)), ((), ())), preferred_element_type=F32)


def contract_first(a, b):
    return lax.dot_general(a, b, (((0,), (0,)), ((), ())), preferred_element_type=F32)


def fold(v):
    return jnp.sum(v.reshape(v.shape[0] // 8, 8, v.shape[1]), axis=0)


def kernel(
    images, texts, positives, log_scale, bias,
    image_grad, text_grad, answer,
    raw, unit, factor, total, held, result, sums, share,
    load_sem, link_send, link_recv, pass_send, pass_recv, pair_send, pair_recv,
    skip_send, skip_recv, share_send, share_recv, out_sem, go_sem,
):
    k = lax.axis_index("blk")
    p = lax.axis_index("dp")
    core = lax.rem(k, 2)
    odd = lax.rem(k // 2, 2)
    pair = k + 1 - 2 * core
    skip = lax.rem(k - 3 + 6 * core + N_BLK, N_BLK)

    def load(side):
        return pltpu.make_async_copy((images, texts)[side], raw.at[side], load_sem.at[side])

    load(1).start()
    load(0).start()

    def group(level, i):
        if level == 0 or level == 6:
            return (pair, p)
        if level == 1 or level == 5:
            return (lax.rem(k + 6 - 12 * odd + N_BLK, N_BLK), p)
        if level == 2:
            return (lax.rem(k + N_BLK // 2, N_BLK), p + 1 - 2 * lax.rem(p, 2))
        if level == 3:
            return (lax.rem(k + 4 * i, N_BLK), p)
        return (k, lax.rem(p + 2 * i, N_DP))

    barrier = pltpu.get_barrier_semaphore()
    greeted = [(lax.rem(k + 2, N_BLK), p), (lax.rem(k - 2 + N_BLK, N_BLK), p), (pair, p), (skip, p)]
    for device in greeted:
        pl.semaphore_signal(barrier, inc=1, device_id=device, device_id_type=MESH)
    lead = 1 - core
    hub = lead * odd

    @pl.when(lead == 1)
    def _():
        pl.semaphore_signal(barrier, inc=1, device_id=group(1, 1), device_id_type=MESH)

    @pl.when(hub == 1)
    def _():
        for level in MIDDLE:
            for i in others(level):
                pl.semaphore_signal(barrier, inc=1, device_id=group(level, i), device_id_type=MESH)

    greetings = len(greeted) + lead + hub * sum(len(others(level)) for level in MIDDLE)

    def link(t):
        second = t // PIECES
        start = pl.multiple_of(PIECE * lax.rem(t, PIECES), PIECE)
        place = pl.multiple_of(2 * PIECE * t, PIECE)
        return pltpu.make_async_remote_copy(
            src_ref=unit.at[1 - second, pl.ds(start, PIECE)],
            dst_ref=held.at[pl.ds(place, PIECE)],
            send_sem=link_send.at[t],
            recv_sem=link_recv.at[t],
            device_id=(lax.rem(k + 2 - 4 * second + N_BLK, N_BLK), p),
            device_id_type=MESH,
        )

    def hand_on(t):
        place = pl.multiple_of(2 * PIECE * t, PIECE)
        return pltpu.make_async_remote_copy(
            src_ref=held.at[pl.ds(place, PIECE)],
            dst_ref=held.at[pl.ds(place + PIECE, PIECE)],
            send_sem=pass_send.at[t],
            recv_sem=pass_recv.at[t],
            device_id=(pair, p),
            device_id_type=MESH,
        )

    def to_pair(q):
        start = pl.multiple_of(TILE * q, TILE)
        return pltpu.make_async_remote_copy(
            src_ref=unit.at[1 - core, pl.ds(start, TILE)],
            dst_ref=held.at[pl.ds(PARTNER + start, TILE)],
            send_sem=pair_send.at[q],
            recv_sem=pair_recv.at[q],
            device_id=(pair, p),
            device_id_type=MESH,
        )

    def send_pair():
        for q in range(4):
            to_pair(q).start()

    def to_skip(q):
        start = pl.multiple_of(TILE * q, TILE)
        return pltpu.make_async_remote_copy(
            src_ref=unit.at[core, pl.ds(start, TILE)],
            dst_ref=held.at[pl.ds(SKIP + start, TILE)],
            send_sem=skip_send.at[q],
            recv_sem=skip_recv.at[q],
            device_id=(skip, p),
            device_id_type=MESH,
        )

    def normalize(side, j):
        rows = pl.ds(pl.multiple_of(PIECE * j, PIECE), PIECE)
        full = raw[side, rows, :].astype(F32)
        scaler = lax.rsqrt(jnp.sum(full * full, axis=-1, keepdims=True) + 1e-06)
        unit[side, rows, :] = (full * scaler).astype(BF16)
        factor[side, rows, :] = jnp.broadcast_to(scaler, (PIECE, 128))

    load(1).wait()
    normalize(1, 0)
    pl.semaphore_wait(barrier, greetings)
    link(0).start()

    @pl.loop(1, PIECES)
    def _(j):
        normalize(1, j)
        link(j).start()

    pl.when(core == 0)(send_pair)
    load(0).wait()

    @pl.loop(0, PIECES)
    def _(j):
        normalize(0, j)

    pl.when(core == 1)(send_pair)

    def send_skip():
        for q in range(4):
            to_skip(q).start()

    pl.when(odd * core == 0)(send_skip)

    @pl.when(odd == 1)
    def _():
        @pl.loop(PIECES, STEPS)
        def _(t):
            link(t).start()

    scale = jnp.exp(jnp.full((1, 128), log_scale[0], F32))
    shift = bias[0]
    sums[...] = jnp.zeros_like(sums)

    def count(weight, loss, logit, coeff):
        sums[0] += weight * fold(loss)
        sums[1] += weight * fold(logit)
        sums[2] += weight * fold(coeff)

    @pl.loop(0, ROWS // TILE)
    def _(c):
        cols = pl.ds(pl.multiple_of(TILE * c, TILE), TILE)
        rows = unit[0, cols, :]
        wanted = positives[:, cols]
        halves = []
        for h in range(2):
            part = pl.ds(HALF * h, HALF)
            product = scale * contract_last(unit[1, part, :], rows)
            logits = product + shift
            match = lax.broadcasted_iota(jnp.int32, (HALF, TILE), 0) + HALF * h == wanted
            odds = jnp.exp(jnp.where(match, -logits, logits))
            chance = odds / (1.0 + odds)
            coeff = jnp.where(match, -chance, chance)
            count(1.0, jnp.log1p(odds), coeff * product, coeff)
            coeff = coeff.astype(BF16)
            halves.append(coeff)
            term = jnp.dot(coeff, rows, preferred_element_type=F32)

            @pl.when(c == 0)
            def _():
                total[1, part, :] = term

            @pl.when(c > 0)
            def _():
                total[1, part, :] += term

        total[0, cols, :] = contract_first(jnp.concatenate(halves, axis=0), unit[1])

    def work(side, place, weight):
        other = held[pl.ds(pl.multiple_of(place, TILE), TILE), :]
        for h in range(2):
            part = pl.ds(HALF * h, HALF)
            product = scale * contract_last(unit[side, part, :], other)
            odds = jnp.exp(product + shift)
            coeff = odds / (1.0 + odds)
            if weight is not None:
                count(weight, jnp.log1p(odds), coeff * product, coeff)
            total[side, part, :] += jnp.dot(coeff.astype(BF16), other, preferred_element_type=F32)

    lane = lax.broadcasted_iota(jnp.int32, (8, 128), 1)

    def exchange(level, i):
        return pltpu.make_async_remote_copy(
            src_ref=share.at[level, 0],
            dst_ref=share.at[level, i],
            send_sem=share_send.at[level, i - 1],
            recv_sem=share_recv.at[level, i - 1],
            device_id=group(level, i),
            device_id_type=MESH,
        )

    def gathered(level):
        for i in others(level):
            exchange(level, i).wait_recv()
        parts = [share[level, i] for i in range(len(others(level)) + 1)]
        while len(parts) > 1:
            half = len(parts) // 2
            parts = [parts[i] + parts[i + half] for i in range(half)]
        return parts[0]

    def send_share(level, value):
        share[level, 0] = value
        for i in others(level):
            exchange(level, i).start()

    def arrive(t):
        link(t).wait_recv()
        hand_on(t).start()

    def use(t, weight):
        hand_on(t).wait_recv()
        work(t // PIECES, 2 * PIECE * t, weight)

    ahead = (lax.rem(k + 2, N_BLK), p)

    @pl.loop(0, STEPS - 2)
    def _(t):
        arrive(t)

        @pl.when((odd == 0) & (t == PIECES - 1))
        def _():
            pl.semaphore_wait(go_sem, 1)

            @pl.loop(PIECES, STEPS)
            def _(i):
                link(i).start()

        pl.when((odd * core == 1) & (t == PIECES - 1))(send_skip)

        @pl.when((lead == 1) & (t == PIECES + 1))
        def _():
            share[1, 0] = gathered(0)
            pl.when(odd == 0)(lambda: exchange(1, 1).start())

        @pl.when(t > 0)
        def _():
            use(t - 1, jnp.where(t <= PIECES, 1.0, 0.0).astype(F32))

        @pl.when((odd == 1) & (t == PIECES - 2))
        def _():
            pl.semaphore_signal(go_sem, inc=1, device_id=ahead, device_id_type=MESH)

        second = t // PIECES
        q = t - 4 - 5 * second

        @pl.when((q >= 0) & (q < 4))
        def _():
            near = core == second
            pl.when(near)(lambda: to_pair(q).wait_recv())
            pl.when(jnp.logical_not(near))(lambda: to_skip(q).wait_recv())
            place = PARTNER + ROWS * (core + second - 2 * core * second)
            work(1 - second, place + TILE * q, 1.0 - second.astype(F32))

        @pl.when(t == PIECES)
        def _():
            value = jnp.zeros((8, 128), F32)
            for i in range(3):
                value = jnp.where(lane == i, jnp.sum(sums[i]), value)
            share[0, 0] = value
            pl.when(core == 1)(lambda: exchange(0, 1).start())

        for level in MIDDLE:
            @pl.when((hub == 1) & (t == PIECES - 1 + level))
            def _():
                send_share(level, gathered(level - 1))

        @pl.when((hub == 1) & (t == PIECES + 4))
        def _():
            value = gathered(4)
            send_share(5, value)
            send_share(6, value)

    def leave(side, j):
        rows = pl.ds(pl.multiple_of(PIECE * j, PIECE), PIECE)
        return pltpu.make_async_copy(
            result.at[side, rows], (image_grad, text_grad)[side].at[rows], out_sem.at[side, j]
        )

    def finish(side, j):
        rows = pl.ds(pl.multiple_of(PIECE * j, PIECE), PIECE)
        full = raw[side, rows, :].astype(F32)
        grad = total[side, rows, :]
        scaler = factor[side, rows, 0:1]
        inner = scaler * scaler * jnp.sum(full * grad, axis=-1, keepdims=True)
        result[side, rows, :] = (scale[:, 0:1] * scaler * (grad - full * inner)).astype(BF16)
        leave(side, j).start()

    arrive(STEPS - 2)
    use(STEPS - 3, None)

    @pl.loop(0, PIECES)
    def _(j):
        finish(0, j)

    use(STEPS - 2, None)

    @pl.when((lead == 1) & (odd == 0))
    def _():
        exchange(5, 1).wait_recv()
        send_share(6, share[5, 1])

    arrive(STEPS - 1)
    use(STEPS - 1, None)

    @pl.loop(0, PIECES)
    def _(j):
        finish(1, j)

    @pl.when(core == 1)
    def _():
        exchange(6, 1).wait_recv()
        share[6, 0] = share[6, 1]

    found = share[6, 0]
    for i in range(3):
        answer[i] = jnp.max(jnp.where(lane == i, found, -jnp.inf)) / COUNT
    for q in range(4):
        to_pair(q).wait_send()
        to_skip(q).wait_send()
    pl.when(core == 1)(lambda: exchange(0, 1).wait_send())
    pl.when(lead == 1)(lambda: exchange(6, 1).wait_send())
    pl.when(lead * (1 - odd) == 1)(lambda: exchange(1, 1).wait_send())

    @pl.when(hub == 1)
    def _():
        for level in (*MIDDLE, 5):
            for i in others(level):
                exchange(level, i).wait_send()

    @pl.loop(0, STEPS)
    def _(t):
        link(t).wait_send()
        hand_on(t).wait_send()

    @pl.loop(0, PIECES)
    def _(j):
        leave(0, j).wait()
        leave(1, j).wait()


def write(image, text, answer, image_grad, text_grad, totals, rows_held, totals_held, load_sem, store_sem):
    loads = [pltpu.make_async_copy(answer, totals_held, load_sem.at[2, 0])]
    stores = [pltpu.make_async_copy(totals_held, totals, store_sem.at[2, 0])]
    for i, (source, target) in enumerate(((image, image_grad), (text, text_grad))):
        for j in range(4):
            rows = pl.ds(TILE * j, TILE)
            loads.append(pltpu.make_async_copy(source.at[rows], rows_held.at[i, rows], load_sem.at[i, j]))
            stores.append(pltpu.make_async_copy(rows_held.at[i, rows], target.at[rows], store_sem.at[i, j]))
    for load in loads:
        load.start()
    for load, store in zip(loads, stores):
        load.wait()
        store.start()
    for store in stores:
        store.wait()


def body(images, texts, positives, log_scale, bias):
    hbm = pl.BlockSpec(memory_space=pltpu.HBM)
    vmem = pl.BlockSpec(memory_space=pltpu.VMEM)
    smem = pl.BlockSpec(memory_space=pltpu.SMEM)
    dma = pltpu.SemaphoreType.DMA
    grad = jax.ShapeDtypeStruct((ROWS, WIDTH), BF16)
    three = jax.ShapeDtypeStruct((3,), F32)
    image, text, answer = pl.pallas_call(
        kernel,
        out_shape=(grad, grad, three),
        in_specs=[hbm, hbm, vmem, smem, smem],
        out_specs=(hbm, hbm, smem),
        scratch_shapes=[
            pltpu.VMEM((2, ROWS, WIDTH), BF16),
            pltpu.VMEM((2, ROWS, WIDTH), BF16),
            pltpu.VMEM((2, ROWS, 128), F32),
            pltpu.VMEM((2, ROWS, WIDTH), F32),
            pltpu.VMEM((SKIP + ROWS, WIDTH), BF16),
            pltpu.VMEM((2, ROWS, WIDTH), BF16),
            pltpu.VMEM((3, 8, 128), F32),
            pltpu.VMEM((LEVELS, 8, 8, 128), F32),
            dma((2,)),
            dma((STEPS,)),
            dma((STEPS,)),
            dma((STEPS,)),
            dma((STEPS,)),
            dma((4,)),
            dma((4,)),
            dma((4,)),
            dma((4,)),
            dma((LEVELS, 7)),
            dma((LEVELS, 7)),
            dma((2, PIECES)),
            pltpu.SemaphoreType.REGULAR,
        ],
        compiler_params=pltpu.CompilerParams(
            collective_id=0, has_side_effects=True, vmem_limit_bytes=58 << 20
        ),
        cost_estimate=pl.CostEstimate(
            flops=15 * 2 * ROWS * ROWS * WIDTH, bytes_accessed=4 * ROWS * WIDTH * 2, transcendentals=0
        ),
    )(images, texts, positives, log_scale, bias)
    return pl.pallas_call(
        write,
        out_shape=(grad, grad, three),
        in_specs=[hbm, hbm, hbm],
        out_specs=(hbm, hbm, hbm),
        scratch_shapes=[
            pltpu.VMEM((2, ROWS, WIDTH), BF16),
            pltpu.SMEM((3,), F32),
            dma((3, 4)),
            dma((3, 4)),
        ],
        compiler_params=pltpu.CompilerParams(vmem_limit_bytes=60 << 20),
    )(image, text, answer)


def solution(mesh):
    return jax.shard_map(
        body,
        mesh=mesh,
        in_specs=(P(("blk", "dp"), None), P(("blk", "dp"), None), P(("blk", "dp"), None), P(), P()),
        out_specs=(P(("blk", "dp"), None), P(("blk", "dp"), None), P()),
        check_vma=False,
    )
```

```python
import jax
import jax.numpy as jnp
from jax import lax
from jax.experimental import pallas as pl
from jax.experimental.pallas import tpu as pltpu
from jax.sharding import PartitionSpec as P

MESH = pl.DeviceIdType.MESH
BF16 = jnp.bfloat16
F32 = jnp.float32

ROWS = 512
WIDTH = 1152
COUNT = 131072.0
N_BLK = 32
N_DP = 8
PIECE = 64
PIECES = ROWS // PIECE
STEPS = 2 * PIECES
TILE = 128
HALF = 256
PARTNER = STEPS * 2 * PIECE
SKIP = PARTNER + ROWS


LEVELS = 7
MIDDLE = (2, 3, 4)


def others(level):
    return range(1, (2, 2, 2, 8, 4, 2, 2)[level])


def contract_last(a, b):
    return lax.dot_general(a, b, (((1,), (1,)), ((), ())), preferred_element_type=F32)


def contract_first(a, b):
    return lax.dot_general(a, b, (((0,), (0,)), ((), ())), preferred_element_type=F32)


def fold(v):
    return jnp.sum(v.reshape(v.shape[0] // 8, 8, v.shape[1]), axis=0)


def kernel(
    images, texts, positives_in, log_scale_in, bias_in,
    image_grad, text_grad, answer_out,
    positives, log_scale, bias, answer, raw, unit, factor, total, held, result, sums, share,
    load_sem, link_send, link_recv, pass_send, pass_recv, pair_send, pair_recv,
    skip_send, skip_recv, share_send, share_recv, out_sem, answer_sem, go_sem,
):
    k = lax.axis_index("blk")
    p = lax.axis_index("dp")
    core = lax.rem(k, 2)
    odd = lax.rem(k // 2, 2)
    pair = k + 1 - 2 * core
    skip = lax.rem(k - 3 + 6 * core + N_BLK, N_BLK)

    def load(side):
        return pltpu.make_async_copy((images, texts)[side], raw.at[side], load_sem.at[side])

    small = [
        pltpu.make_async_copy(source, target, load_sem.at[2 + i])
        for i, (source, target) in enumerate(
            ((positives_in, positives), (log_scale_in, log_scale), (bias_in, bias))
        )
    ]
    load(1).start()
    load(0).start()
    for copy in small:
        copy.start()

    def group(level, i):
        if level == 0 or level == 6:
            return (pair, p)
        if level == 1 or level == 5:
            return (lax.rem(k + 6 - 12 * odd + N_BLK, N_BLK), p)
        if level == 2:
            return (lax.rem(k + N_BLK // 2, N_BLK), p + 1 - 2 * lax.rem(p, 2))
        if level == 3:
            return (lax.rem(k + 4 * i, N_BLK), p)
        return (k, lax.rem(p + 2 * i, N_DP))

    barrier = pltpu.get_barrier_semaphore()
    greeted = [(lax.rem(k + 2, N_BLK), p), (lax.rem(k - 2 + N_BLK, N_BLK), p), (pair, p), (skip, p)]
    for device in greeted:
        pl.semaphore_signal(barrier, inc=1, device_id=device, device_id_type=MESH)
    lead = 1 - core
    hub = lead * odd

    @pl.when(lead == 1)
    def _():
        pl.semaphore_signal(barrier, inc=1, device_id=group(1, 1), device_id_type=MESH)

    @pl.when(hub == 1)
    def _():
        for level in MIDDLE:
            for i in others(level):
                pl.semaphore_signal(barrier, inc=1, device_id=group(level, i), device_id_type=MESH)

    greetings = len(greeted) + lead + hub * sum(len(others(level)) for level in MIDDLE)

    def link(t):
        second = t // PIECES
        start = pl.multiple_of(PIECE * lax.rem(t, PIECES), PIECE)
        place = pl.multiple_of(2 * PIECE * t, PIECE)
        return pltpu.make_async_remote_copy(
            src_ref=unit.at[1 - second, pl.ds(start, PIECE)],
            dst_ref=held.at[pl.ds(place, PIECE)],
            send_sem=link_send.at[t],
            recv_sem=link_recv.at[t],
            device_id=(lax.rem(k + 2 - 4 * second + N_BLK, N_BLK), p),
            device_id_type=MESH,
        )

    def hand_on(t):
        place = pl.multiple_of(2 * PIECE * t, PIECE)
        return pltpu.make_async_remote_copy(
            src_ref=held.at[pl.ds(place, PIECE)],
            dst_ref=held.at[pl.ds(place + PIECE, PIECE)],
            send_sem=pass_send.at[t],
            recv_sem=pass_recv.at[t],
            device_id=(pair, p),
            device_id_type=MESH,
        )

    def to_pair(q):
        start = pl.multiple_of(TILE * q, TILE)
        return pltpu.make_async_remote_copy(
            src_ref=unit.at[1 - core, pl.ds(start, TILE)],
            dst_ref=held.at[pl.ds(PARTNER + start, TILE)],
            send_sem=pair_send.at[q],
            recv_sem=pair_recv.at[q],
            device_id=(pair, p),
            device_id_type=MESH,
        )

    def send_pair():
        for q in range(4):
            to_pair(q).start()

    def to_skip(q):
        start = pl.multiple_of(TILE * q, TILE)
        return pltpu.make_async_remote_copy(
            src_ref=unit.at[core, pl.ds(start, TILE)],
            dst_ref=held.at[pl.ds(SKIP + start, TILE)],
            send_sem=skip_send.at[q],
            recv_sem=skip_recv.at[q],
            device_id=(skip, p),
            device_id_type=MESH,
        )

    def normalize(side, j):
        rows = pl.ds(pl.multiple_of(PIECE * j, PIECE), PIECE)
        full = raw[side, rows, :].astype(F32)
        scaler = lax.rsqrt(jnp.sum(full * full, axis=-1, keepdims=True) + 1e-06)
        unit[side, rows, :] = (full * scaler).astype(BF16)
        factor[side, rows, :] = jnp.broadcast_to(scaler, (PIECE, 128))

    load(1).wait()
    normalize(1, 0)
    pl.semaphore_wait(barrier, greetings)
    link(0).start()

    @pl.loop(1, PIECES)
    def _(j):
        normalize(1, j)
        link(j).start()

    pl.when(core == 0)(send_pair)
    load(0).wait()

    @pl.loop(0, PIECES)
    def _(j):
        normalize(0, j)

    pl.when(core == 1)(send_pair)

    def send_skip():
        for q in range(4):
            to_skip(q).start()

    pl.when(odd * core == 0)(send_skip)

    @pl.when(odd == 1)
    def _():
        @pl.loop(PIECES, STEPS)
        def _(t):
            link(t).start()

    for copy in small:
        copy.wait()
    scale = jnp.exp(jnp.full((1, 128), log_scale[0], F32))
    shift = bias[0]
    sums[...] = jnp.zeros_like(sums)

    def count(weight, loss, logit, coeff):
        sums[0] += weight * fold(loss)
        sums[1] += weight * fold(logit)
        sums[2] += weight * fold(coeff)

    @pl.loop(0, ROWS // TILE)
    def _(c):
        cols = pl.ds(pl.multiple_of(TILE * c, TILE), TILE)
        rows = unit[0, cols, :]
        wanted = positives[:, cols]
        halves = []
        for h in range(2):
            part = pl.ds(HALF * h, HALF)
            product = scale * contract_last(unit[1, part, :], rows)
            logits = product + shift
            match = lax.broadcasted_iota(jnp.int32, (HALF, TILE), 0) + HALF * h == wanted
            odds = jnp.exp(jnp.where(match, -logits, logits))
            chance = odds / (1.0 + odds)
            coeff = jnp.where(match, -chance, chance)
            count(1.0, jnp.log1p(odds), coeff * product, coeff)
            coeff = coeff.astype(BF16)
            halves.append(coeff)
            term = jnp.dot(coeff, rows, preferred_element_type=F32)

            @pl.when(c == 0)
            def _():
                total[1, part, :] = term

            @pl.when(c > 0)
            def _():
                total[1, part, :] += term

        total[0, cols, :] = contract_first(jnp.concatenate(halves, axis=0), unit[1])

    def work_half(side, other, weight, h):
        part = pl.ds(HALF * h, HALF)
        product = scale * contract_last(unit[side, part, :], other)
        odds = jnp.exp(product + shift)
        coeff = odds / (1.0 + odds)
        if weight is not None:
            count(weight, jnp.log1p(odds), coeff * product, coeff)
        total[side, part, :] += jnp.dot(coeff.astype(BF16), other, preferred_element_type=F32)

    def work(side, place, weight):
        other = held[pl.ds(pl.multiple_of(place, TILE), TILE), :]
        for h in range(2):
            work_half(side, other, weight, h)

    lane = lax.broadcasted_iota(jnp.int32, (8, 128), 1)

    def exchange(level, i):
        return pltpu.make_async_remote_copy(
            src_ref=share.at[level, 0],
            dst_ref=share.at[level, i],
            send_sem=share_send.at[level, i - 1],
            recv_sem=share_recv.at[level, i - 1],
            device_id=group(level, i),
            device_id_type=MESH,
        )

    def gathered(level):
        for i in others(level):
            exchange(level, i).wait_recv()
        parts = [share[level, i] for i in range(len(others(level)) + 1)]
        while len(parts) > 1:
            half = len(parts) // 2
            parts = [parts[i] + parts[i + half] for i in range(half)]
        return parts[0]

    def send_share(level, value):
        share[level, 0] = value
        for i in others(level):
            exchange(level, i).start()

    def arrive(t):
        link(t).wait_recv()
        hand_on(t).start()

    def use(t, weight):
        hand_on(t).wait_recv()
        work(t // PIECES, 2 * PIECE * t, weight)

    ahead = (lax.rem(k + 2, N_BLK), p)

    @pl.loop(0, STEPS - 2)
    def _(t):
        arrive(t)

        @pl.when((odd == 0) & (t == PIECES - 1))
        def _():
            pl.semaphore_wait(go_sem, 1)

            @pl.loop(PIECES, STEPS)
            def _(i):
                link(i).start()

        pl.when((odd * core == 1) & (t == PIECES - 1))(send_skip)

        @pl.when((lead == 1) & (t == PIECES + 1))
        def _():
            share[1, 0] = gathered(0)
            pl.when(odd == 0)(lambda: exchange(1, 1).start())

        @pl.when(t > 0)
        def _():
            use(t - 1, jnp.where(t <= PIECES, 1.0, 0.0).astype(F32))

        @pl.when((odd == 1) & (t == PIECES - 2))
        def _():
            pl.semaphore_signal(go_sem, inc=1, device_id=ahead, device_id_type=MESH)

        second = t // PIECES
        q = t - 4 - 5 * second

        @pl.when((q >= 0) & (q < 4))
        def _():
            near = core == second
            pl.when(near)(lambda: to_pair(q).wait_recv())
            pl.when(jnp.logical_not(near))(lambda: to_skip(q).wait_recv())
            place = PARTNER + ROWS * (core + second - 2 * core * second)
            work(1 - second, place + TILE * q, 1.0 - second.astype(F32))

        @pl.when(t == PIECES)
        def _():
            value = jnp.zeros((8, 128), F32)
            for i in range(3):
                value = jnp.where(lane == i, jnp.sum(sums[i]), value)
            share[0, 0] = value
            pl.when(core == 1)(lambda: exchange(0, 1).start())

        for level in MIDDLE:
            @pl.when((hub == 1) & (t == PIECES - 1 + level))
            def _():
                send_share(level, gathered(level - 1))

        @pl.when((hub == 1) & (t == PIECES + 4))
        def _():
            value = gathered(4)
            send_share(5, value)
            send_share(6, value)

    def leave(side, j):
        rows = pl.ds(pl.multiple_of(PIECE * j, PIECE), PIECE)
        return pltpu.make_async_copy(
            result.at[side, rows], (image_grad, text_grad)[side].at[rows], out_sem.at[side, j]
        )

    def finish(side, j):
        rows = pl.ds(pl.multiple_of(PIECE * j, PIECE), PIECE)
        full = raw[side, rows, :].astype(F32)
        grad = total[side, rows, :]
        scaler = factor[side, rows, 0:1]
        inner = scaler * scaler * jnp.sum(full * grad, axis=-1, keepdims=True)
        result[side, rows, :] = (scale[:, 0:1] * scaler * (grad - full * inner)).astype(BF16)
        leave(side, j).start()

    arrive(STEPS - 2)
    use(STEPS - 3, None)

    @pl.loop(0, PIECES)
    def _(j):
        finish(0, j)

    use(STEPS - 2, None)

    @pl.when((lead == 1) & (odd == 0))
    def _():
        exchange(5, 1).wait_recv()
        send_share(6, share[5, 1])

    arrive(STEPS - 1)
    hand_on(STEPS - 1).wait_recv()
    other = held[2 * PIECE * (STEPS - 1) : 2 * PIECE * STEPS, :]
    for h in range(2):
        work_half(1, other, None, h)
        for j in range(PIECES // 2):
            finish(1, PIECES // 2 * h + j)

    @pl.when(core == 1)
    def _():
        exchange(6, 1).wait_recv()
        share[6, 0] = share[6, 1]

    found = share[6, 0]
    for i in range(3):
        answer[i] = jnp.max(jnp.where(lane == i, found, -jnp.inf)) / COUNT
    leave_answer = pltpu.make_async_copy(answer, answer_out, answer_sem)
    leave_answer.start()
    for q in range(4):
        to_pair(q).wait_send()
        to_skip(q).wait_send()
    pl.when(core == 1)(lambda: exchange(0, 1).wait_send())
    pl.when(lead == 1)(lambda: exchange(6, 1).wait_send())
    pl.when(lead * (1 - odd) == 1)(lambda: exchange(1, 1).wait_send())

    @pl.when(hub == 1)
    def _():
        for level in (*MIDDLE, 5):
            for i in others(level):
                exchange(level, i).wait_send()

    @pl.loop(0, STEPS)
    def _(t):
        link(t).wait_send()
        hand_on(t).wait_send()

    @pl.loop(0, PIECES)
    def _(j):
        leave(0, j).wait()
        leave(1, j).wait()

    leave_answer.wait()


def write(image, text, answer, image_grad, text_grad, totals, rows_held, totals_held, load_sem, store_sem):
    loads = [pltpu.make_async_copy(answer, totals_held, load_sem.at[2, 0])]
    stores = [pltpu.make_async_copy(totals_held, totals, store_sem.at[2, 0])]
    for i, (source, target) in enumerate(((image, image_grad), (text, text_grad))):
        for j in range(4):
            rows = pl.ds(TILE * j, TILE)
            loads.append(pltpu.make_async_copy(source.at[rows], rows_held.at[i, rows], load_sem.at[i, j]))
            stores.append(pltpu.make_async_copy(rows_held.at[i, rows], target.at[rows], store_sem.at[i, j]))
    for load in loads:
        load.start()
    for load, store in zip(loads, stores):
        load.wait()
        store.start()
    for store in stores:
        store.wait()


def body(images, texts, positives, log_scale, bias):
    hbm = pl.BlockSpec(memory_space=pltpu.HBM)
    dma = pltpu.SemaphoreType.DMA
    grad = jax.ShapeDtypeStruct((ROWS, WIDTH), BF16)
    three = jax.ShapeDtypeStruct((3,), F32)
    image, text, answer = pl.pallas_call(
        kernel,
        out_shape=(grad, grad, three),
        in_specs=[hbm, hbm, hbm, hbm, hbm],
        out_specs=(hbm, hbm, hbm),
        scratch_shapes=[
            pltpu.VMEM((1, ROWS), jnp.int32),
            pltpu.SMEM((1,), F32),
            pltpu.SMEM((1,), F32),
            pltpu.SMEM((3,), F32),
            pltpu.VMEM((2, ROWS, WIDTH), BF16),
            pltpu.VMEM((2, ROWS, WIDTH), BF16),
            pltpu.VMEM((2, ROWS, 128), F32),
            pltpu.VMEM((2, ROWS, WIDTH), F32),
            pltpu.VMEM((SKIP + ROWS, WIDTH), BF16),
            pltpu.VMEM((2, ROWS, WIDTH), BF16),
            pltpu.VMEM((3, 8, 128), F32),
            pltpu.VMEM((LEVELS, 8, 8, 128), F32),
            dma((5,)),
            dma((STEPS,)),
            dma((STEPS,)),
            dma((STEPS,)),
            dma((STEPS,)),
            dma((4,)),
            dma((4,)),
            dma((4,)),
            dma((4,)),
            dma((LEVELS, 7)),
            dma((LEVELS, 7)),
            dma((2, PIECES)),
            dma,
            pltpu.SemaphoreType.REGULAR,
        ],
        compiler_params=pltpu.CompilerParams(
            collective_id=0, has_side_effects=True, vmem_limit_bytes=58 << 20
        ),
        cost_estimate=pl.CostEstimate(
            flops=15 * 2 * ROWS * ROWS * WIDTH, bytes_accessed=4 * ROWS * WIDTH * 2, transcendentals=0
        ),
    )(images, texts, positives, log_scale, bias)
    return pl.pallas_call(
        write,
        out_shape=(grad, grad, three),
        in_specs=[hbm, hbm, hbm],
        out_specs=(hbm, hbm, hbm),
        scratch_shapes=[
            pltpu.VMEM((2, ROWS, WIDTH), BF16),
            pltpu.SMEM((3,), F32),
            dma((3, 4)),
            dma((3, 4)),
        ],
        compiler_params=pltpu.CompilerParams(vmem_limit_bytes=60 << 20),
    )(image, text, answer)


def solution(mesh):
    return jax.shard_map(
        body,
        mesh=mesh,
        in_specs=(P(("blk", "dp"), None), P(("blk", "dp"), None), P(("blk", "dp"), None), P(), P()),
        out_specs=(P(("blk", "dp"), None), P(("blk", "dp"), None), P()),
        check_vma=False,
    )
```

```python
import jax
import jax.numpy as jnp
from jax import lax
from jax.experimental import pallas as pl
from jax.experimental.pallas import tpu as pltpu
from jax.sharding import PartitionSpec as P

MESH = pl.DeviceIdType.MESH
BF16 = jnp.bfloat16
F32 = jnp.float32

ROWS = 512
WIDTH = 1152
COUNT = 131072.0
N_BLK = 32
N_DP = 8
PIECE = 64
PIECES = ROWS // PIECE
STEPS = 2 * PIECES
TILE = 128
HALF = 256
PARTNER = STEPS * 2 * PIECE
SKIP = PARTNER + ROWS


LEVELS = 7
MIDDLE = (2, 3, 4)


def others(level):
    return range(1, (2, 2, 2, 8, 4, 2, 2)[level])


def contract_last(a, b):
    return lax.dot_general(a, b, (((1,), (1,)), ((), ())), preferred_element_type=F32)


def contract_first(a, b):
    return lax.dot_general(a, b, (((0,), (0,)), ((), ())), preferred_element_type=F32)


def fold(v):
    return jnp.sum(v.reshape(v.shape[0] // 8, 8, v.shape[1]), axis=0)


def kernel(
    images, texts, positives_in, log_scale_in, bias_in,
    image_grad, text_grad, answer_out,
    positives, log_scale, bias, answer, raw, unit, factor, total, held, result, sums, share,
    load_sem, link_send, link_recv, pass_send, pass_recv, pair_send, pair_recv,
    skip_send, skip_recv, share_send, share_recv, out_sem, answer_sem, go_sem,
):
    k = lax.axis_index("blk")
    p = lax.axis_index("dp")
    core = lax.rem(k, 2)
    odd = lax.rem(k // 2, 2)
    pair = k + 1 - 2 * core
    skip = lax.rem(k - 3 + 6 * core + N_BLK, N_BLK)

    def load(side):
        return pltpu.make_async_copy((images, texts)[side], raw.at[side], load_sem.at[side])

    small = [
        pltpu.make_async_copy(source, target, load_sem.at[2 + i])
        for i, (source, target) in enumerate(
            ((positives_in, positives), (log_scale_in, log_scale), (bias_in, bias))
        )
    ]
    load(1).start()
    load(0).start()
    for copy in small:
        copy.start()

    def group(level, i):
        if level == 0 or level == 6:
            return (pair, p)
        if level == 1 or level == 5:
            return (lax.rem(k + 6 - 12 * odd + N_BLK, N_BLK), p)
        if level == 2:
            return (lax.rem(k + N_BLK // 2, N_BLK), p + 1 - 2 * lax.rem(p, 2))
        if level == 3:
            return (lax.rem(k + 4 * i, N_BLK), p)
        return (k, lax.rem(p + 2 * i, N_DP))

    barrier = pltpu.get_barrier_semaphore()
    greeted = [(lax.rem(k + 2, N_BLK), p), (lax.rem(k - 2 + N_BLK, N_BLK), p), (pair, p), (skip, p)]
    for device in greeted:
        pl.semaphore_signal(barrier, inc=1, device_id=device, device_id_type=MESH)
    lead = 1 - core
    hub = lead * odd

    @pl.when(lead == 1)
    def _():
        pl.semaphore_signal(barrier, inc=1, device_id=group(1, 1), device_id_type=MESH)

    @pl.when(hub == 1)
    def _():
        for level in MIDDLE:
            for i in others(level):
                pl.semaphore_signal(barrier, inc=1, device_id=group(level, i), device_id_type=MESH)

    greetings = len(greeted) + lead + hub * sum(len(others(level)) for level in MIDDLE)

    def link(t):
        second = t // PIECES
        start = pl.multiple_of(PIECE * lax.rem(t, PIECES), PIECE)
        place = pl.multiple_of(2 * PIECE * t, PIECE)
        return pltpu.make_async_remote_copy(
            src_ref=unit.at[1 - second, pl.ds(start, PIECE)],
            dst_ref=held.at[pl.ds(place, PIECE)],
            send_sem=link_send.at[t],
            recv_sem=link_recv.at[t],
            device_id=(lax.rem(k + 2 - 4 * second + N_BLK, N_BLK), p),
            device_id_type=MESH,
        )

    def hand_on(t):
        place = pl.multiple_of(2 * PIECE * t, PIECE)
        return pltpu.make_async_remote_copy(
            src_ref=held.at[pl.ds(place, PIECE)],
            dst_ref=held.at[pl.ds(place + PIECE, PIECE)],
            send_sem=pass_send.at[t],
            recv_sem=pass_recv.at[t],
            device_id=(pair, p),
            device_id_type=MESH,
        )

    def to_pair(q):
        start = pl.multiple_of(TILE * q, TILE)
        return pltpu.make_async_remote_copy(
            src_ref=unit.at[1 - core, pl.ds(start, TILE)],
            dst_ref=held.at[pl.ds(PARTNER + start, TILE)],
            send_sem=pair_send.at[q],
            recv_sem=pair_recv.at[q],
            device_id=(pair, p),
            device_id_type=MESH,
        )

    def send_pair():
        for q in range(4):
            to_pair(q).start()

    def to_skip(q):
        start = pl.multiple_of(TILE * q, TILE)
        return pltpu.make_async_remote_copy(
            src_ref=unit.at[core, pl.ds(start, TILE)],
            dst_ref=held.at[pl.ds(SKIP + start, TILE)],
            send_sem=skip_send.at[q],
            recv_sem=skip_recv.at[q],
            device_id=(skip, p),
            device_id_type=MESH,
        )

    def normalize(side, j):
        rows = pl.ds(pl.multiple_of(PIECE * j, PIECE), PIECE)
        full = raw[side, rows, :].astype(F32)
        scaler = lax.rsqrt(jnp.sum(full * full, axis=-1, keepdims=True) + 1e-06)
        unit[side, rows, :] = (full * scaler).astype(BF16)
        factor[side, rows, :] = jnp.broadcast_to(scaler, (PIECE, 128))

    load(1).wait()
    normalize(1, 0)
    pl.semaphore_wait(barrier, greetings)
    link(0).start()

    @pl.loop(1, PIECES)
    def _(j):
        normalize(1, j)
        link(j).start()

    pl.when(core == 0)(send_pair)
    load(0).wait()

    @pl.loop(0, PIECES)
    def _(j):
        normalize(0, j)

    pl.when(core == 1)(send_pair)

    def send_skip():
        for q in range(4):
            to_skip(q).start()

    pl.when(odd * core == 0)(send_skip)

    @pl.when(odd == 1)
    def _():
        @pl.loop(PIECES, STEPS)
        def _(t):
            link(t).start()

    for copy in small:
        copy.wait()
    scale = jnp.exp(jnp.full((1, 128), log_scale[0], F32))
    shift = bias[0]
    sums[...] = jnp.zeros_like(sums)

    def count(weight, loss, logit, coeff):
        sums[0] += weight * fold(loss)
        sums[1] += weight * fold(logit)
        sums[2] += weight * fold(coeff)

    @pl.loop(0, ROWS // TILE)
    def _(c):
        cols = pl.ds(pl.multiple_of(TILE * c, TILE), TILE)
        rows = unit[0, cols, :]
        wanted = positives[:, cols]
        halves = []
        for h in range(2):
            part = pl.ds(HALF * h, HALF)
            product = scale * contract_last(unit[1, part, :], rows)
            logits = product + shift
            match = lax.broadcasted_iota(jnp.int32, (HALF, TILE), 0) + HALF * h == wanted
            odds = jnp.exp(jnp.where(match, -logits, logits))
            chance = odds / (1.0 + odds)
            coeff = jnp.where(match, -chance, chance)
            count(1.0, jnp.log1p(odds), coeff * product, coeff)
            coeff = coeff.astype(BF16)
            halves.append(coeff)
            term = jnp.dot(coeff, rows, preferred_element_type=F32)

            @pl.when(c == 0)
            def _():
                total[1, part, :] = term

            @pl.when(c > 0)
            def _():
                total[1, part, :] += term

        total[0, cols, :] = contract_first(jnp.concatenate(halves, axis=0), unit[1])

    def work_half(side, other, weight, h):
        part = pl.ds(HALF * h, HALF)
        product = scale * contract_last(unit[side, part, :], other)
        odds = jnp.exp(product + shift)
        coeff = odds / (1.0 + odds)
        if weight is not None:
            count(weight, jnp.log1p(odds), coeff * product, coeff)
        total[side, part, :] += jnp.dot(coeff.astype(BF16), other, preferred_element_type=F32)

    def work(side, place, weight):
        other = held[pl.ds(pl.multiple_of(place, TILE), TILE), :]
        for h in range(2):
            work_half(side, other, weight, h)

    lane = lax.broadcasted_iota(jnp.int32, (8, 128), 1)

    def exchange(level, i):
        return pltpu.make_async_remote_copy(
            src_ref=share.at[level, 0],
            dst_ref=share.at[level, i],
            send_sem=share_send.at[level, i - 1],
            recv_sem=share_recv.at[level, i - 1],
            device_id=group(level, i),
            device_id_type=MESH,
        )

    def gathered(level):
        for i in others(level):
            exchange(level, i).wait_recv()
        parts = [share[level, i] for i in range(len(others(level)) + 1)]
        while len(parts) > 1:
            half = len(parts) // 2
            parts = [parts[i] + parts[i + half] for i in range(half)]
        return parts[0]

    def send_share(level, value):
        share[level, 0] = value
        for i in others(level):
            exchange(level, i).start()

    def arrive(t):
        link(t).wait_recv()
        hand_on(t).start()

    def use(t, weight):
        hand_on(t).wait_recv()
        work(t // PIECES, 2 * PIECE * t, weight)

    ahead = (lax.rem(k + 2, N_BLK), p)

    @pl.loop(0, STEPS - 2)
    def _(t):
        arrive(t)

        @pl.when((odd == 0) & (t == PIECES - 2))
        def _():
            pl.semaphore_wait(go_sem, 1)

            @pl.loop(PIECES, STEPS)
            def _(i):
                link(i).start()

        pl.when((odd * core == 1) & (t == PIECES - 1))(send_skip)

        @pl.when((lead == 1) & (t == PIECES + 1))
        def _():
            share[1, 0] = gathered(0)
            pl.when(odd == 0)(lambda: exchange(1, 1).start())

        @pl.when(t > 0)
        def _():
            use(t - 1, jnp.where(t <= PIECES, 1.0, 0.0).astype(F32))

        @pl.when((odd == 1) & (t == PIECES - 2))
        def _():
            pl.semaphore_signal(go_sem, inc=1, device_id=ahead, device_id_type=MESH)

        second = t // PIECES
        q = t - 4 - 5 * second

        @pl.when((q >= 0) & (q < 4))
        def _():
            near = core == second
            pl.when(near)(lambda: to_pair(q).wait_recv())
            pl.when(jnp.logical_not(near))(lambda: to_skip(q).wait_recv())
            place = PARTNER + ROWS * (core + second - 2 * core * second)
            work(1 - second, place + TILE * q, 1.0 - second.astype(F32))

        @pl.when(t == PIECES)
        def _():
            value = jnp.zeros((8, 128), F32)
            for i in range(3):
                value = jnp.where(lane == i, jnp.sum(sums[i]), value)
            share[0, 0] = value
            pl.when(core == 1)(lambda: exchange(0, 1).start())

        for level in MIDDLE:
            @pl.when((hub == 1) & (t == PIECES - 1 + level))
            def _():
                send_share(level, gathered(level - 1))

        @pl.when((hub == 1) & (t == PIECES + 4))
        def _():
            value = gathered(4)
            send_share(5, value)
            send_share(6, value)

    def leave(side, j):
        rows = pl.ds(pl.multiple_of(PIECE * j, PIECE), PIECE)
        return pltpu.make_async_copy(
            result.at[side, rows], (image_grad, text_grad)[side].at[rows], out_sem.at[side, j]
        )

    def finish(side, j):
        rows = pl.ds(pl.multiple_of(PIECE * j, PIECE), PIECE)
        full = raw[side, rows, :].astype(F32)
        grad = total[side, rows, :]
        scaler = factor[side, rows, 0:1]
        inner = scaler * scaler * jnp.sum(full * grad, axis=-1, keepdims=True)
        result[side, rows, :] = (scale[:, 0:1] * scaler * (grad - full * inner)).astype(BF16)
        leave(side, j).start()

    arrive(STEPS - 2)
    use(STEPS - 3, None)

    @pl.loop(0, PIECES)
    def _(j):
        finish(0, j)

    use(STEPS - 2, None)

    for q in range(4):
        to_pair(q).wait_send()
        to_skip(q).wait_send()

    @pl.loop(0, STEPS - 2)
    def _(t):
        link(t).wait_send()
        hand_on(t).wait_send()

    @pl.loop(0, PIECES)
    def _(j):
        leave(0, j).wait()

    arrive(STEPS - 1)

    @pl.when((lead == 1) & (odd == 0))
    def _():
        exchange(5, 1).wait_recv()
        send_share(6, share[5, 1])

    hand_on(STEPS - 1).wait_recv()
    other = held[2 * PIECE * (STEPS - 1) : 2 * PIECE * STEPS, :]
    for h in range(2):
        work_half(1, other, None, h)
        for j in range(PIECES // 2):
            finish(1, PIECES // 2 * h + j)

    @pl.when(core == 1)
    def _():
        exchange(6, 1).wait_recv()
        share[6, 0] = share[6, 1]

    found = share[6, 0]
    for i in range(3):
        answer[i] = jnp.max(jnp.where(lane == i, found, -jnp.inf)) / COUNT
    leave_answer = pltpu.make_async_copy(answer, answer_out, answer_sem)
    leave_answer.start()
    pl.when(core == 1)(lambda: exchange(0, 1).wait_send())
    pl.when(lead == 1)(lambda: exchange(6, 1).wait_send())
    pl.when(lead * (1 - odd) == 1)(lambda: exchange(1, 1).wait_send())

    @pl.when(hub == 1)
    def _():
        for level in (*MIDDLE, 5):
            for i in others(level):
                exchange(level, i).wait_send()

    @pl.loop(STEPS - 2, STEPS)
    def _(t):
        link(t).wait_send()
        hand_on(t).wait_send()

    @pl.loop(0, PIECES)
    def _(j):
        leave(1, j).wait()

    leave_answer.wait()


def write(image, text, answer, image_grad, text_grad, totals, rows_held, totals_held, load_sem, store_sem):
    loads = [pltpu.make_async_copy(answer, totals_held, load_sem.at[2, 0])]
    stores = [pltpu.make_async_copy(totals_held, totals, store_sem.at[2, 0])]
    for i, (source, target) in enumerate(((image, image_grad), (text, text_grad))):
        for j in range(4):
            rows = pl.ds(TILE * j, TILE)
            loads.append(pltpu.make_async_copy(source.at[rows], rows_held.at[i, rows], load_sem.at[i, j]))
            stores.append(pltpu.make_async_copy(rows_held.at[i, rows], target.at[rows], store_sem.at[i, j]))
    for load in loads:
        load.start()
    for load, store in zip(loads, stores):
        load.wait()
        store.start()
    for store in stores:
        store.wait()


def body(images, texts, positives, log_scale, bias):
    hbm = pl.BlockSpec(memory_space=pltpu.HBM)
    dma = pltpu.SemaphoreType.DMA
    grad = jax.ShapeDtypeStruct((ROWS, WIDTH), BF16)
    three = jax.ShapeDtypeStruct((3,), F32)
    image, text, answer = pl.pallas_call(
        kernel,
        out_shape=(grad, grad, three),
        in_specs=[hbm, hbm, hbm, hbm, hbm],
        out_specs=(hbm, hbm, hbm),
        scratch_shapes=[
            pltpu.VMEM((1, ROWS), jnp.int32),
            pltpu.SMEM((1,), F32),
            pltpu.SMEM((1,), F32),
            pltpu.SMEM((3,), F32),
            pltpu.VMEM((2, ROWS, WIDTH), BF16),
            pltpu.VMEM((2, ROWS, WIDTH), BF16),
            pltpu.VMEM((2, ROWS, 128), F32),
            pltpu.VMEM((2, ROWS, WIDTH), F32),
            pltpu.VMEM((SKIP + ROWS, WIDTH), BF16),
            pltpu.VMEM((2, ROWS, WIDTH), BF16),
            pltpu.VMEM((3, 8, 128), F32),
            pltpu.VMEM((LEVELS, 8, 8, 128), F32),
            dma((5,)),
            dma((STEPS,)),
            dma((STEPS,)),
            dma((STEPS,)),
            dma((STEPS,)),
            dma((4,)),
            dma((4,)),
            dma((4,)),
            dma((4,)),
            dma((LEVELS, 7)),
            dma((LEVELS, 7)),
            dma((2, PIECES)),
            dma,
            pltpu.SemaphoreType.REGULAR,
        ],
        compiler_params=pltpu.CompilerParams(
            collective_id=0, has_side_effects=True, vmem_limit_bytes=58 << 20
        ),
        cost_estimate=pl.CostEstimate(
            flops=15 * 2 * ROWS * ROWS * WIDTH, bytes_accessed=4 * ROWS * WIDTH * 2, transcendentals=0
        ),
    )(images, texts, positives, log_scale, bias)
    return pl.pallas_call(
        write,
        out_shape=(grad, grad, three),
        in_specs=[hbm, hbm, hbm],
        out_specs=(hbm, hbm, hbm),
        scratch_shapes=[
            pltpu.VMEM((2, ROWS, WIDTH), BF16),
            pltpu.SMEM((3,), F32),
            dma((3, 4)),
            dma((3, 4)),
        ],
        compiler_params=pltpu.CompilerParams(vmem_limit_bytes=60 << 20),
    )(image, text, answer)


def solution(mesh):
    return jax.shard_map(
        body,
        mesh=mesh,
        in_specs=(P(("blk", "dp"), None), P(("blk", "dp"), None), P(("blk", "dp"), None), P(), P()),
        out_specs=(P(("blk", "dp"), None), P(("blk", "dp"), None), P()),
        check_vma=False,
    )
```

```python
import jax
import jax.numpy as jnp
from jax import lax
from jax.experimental import pallas as pl
from jax.experimental.pallas import tpu as pltpu
from jax.sharding import PartitionSpec as P

MESH = pl.DeviceIdType.MESH
BF16 = jnp.bfloat16
F32 = jnp.float32

ROWS = 512
WIDTH = 1152
COUNT = 131072.0
N_BLK = 32
N_DP = 8
PIECE = 64
PIECES = ROWS // PIECE
STEPS = 2 * PIECES
TILE = 128
HALF = 256
PARTNER = STEPS * 2 * PIECE
SKIP = PARTNER + ROWS


LEVELS = 7
MIDDLE = (2, 3, 4)


def others(level):
    return range(1, (2, 2, 2, 8, 4, 2, 2)[level])


def contract_last(a, b):
    return lax.dot_general(a, b, (((1,), (1,)), ((), ())), preferred_element_type=F32)


def contract_first(a, b):
    return lax.dot_general(a, b, (((0,), (0,)), ((), ())), preferred_element_type=F32)


def fold(v):
    return jnp.sum(v.reshape(v.shape[0] // 8, 8, v.shape[1]), axis=0)


def kernel(
    images, texts, positives_in, log_scale_in, bias_in,
    image_grad, text_grad, answer_out,
    positives, log_scale, bias, answer, raw, unit, factor, total, held, result, sums, share,
    load_sem, link_send, link_recv, pass_send, pass_recv, pair_send, pair_recv,
    skip_send, skip_recv, share_send, share_recv, out_sem, answer_sem, go_sem,
):
    k = lax.axis_index("blk")
    p = lax.axis_index("dp")
    core = lax.rem(k, 2)
    odd = lax.rem(k // 2, 2)
    pair = k + 1 - 2 * core
    skip = lax.rem(k - 3 + 6 * core + N_BLK, N_BLK)

    def load(side):
        return pltpu.make_async_copy((images, texts)[side], raw.at[side], load_sem.at[side])

    small = [
        pltpu.make_async_copy(source, target, load_sem.at[2 + i])
        for i, (source, target) in enumerate(
            ((positives_in, positives), (log_scale_in, log_scale), (bias_in, bias))
        )
    ]
    first, rest = pl.ds(0, PIECE), pl.ds(PIECE, ROWS - PIECE)
    load_first = pltpu.make_async_copy(texts.at[first], raw.at[1, first], load_sem.at[5])
    load_rest = pltpu.make_async_copy(texts.at[rest], raw.at[1, rest], load_sem.at[1])
    load_first.start()
    load_rest.start()
    load(0).start()
    for copy in small:
        copy.start()

    def group(level, i):
        if level == 0 or level == 6:
            return (pair, p)
        if level == 1 or level == 5:
            return (lax.rem(k + 6 - 12 * odd + N_BLK, N_BLK), p)
        if level == 2:
            return (lax.rem(k + N_BLK // 2, N_BLK), p + 1 - 2 * lax.rem(p, 2))
        if level == 3:
            return (lax.rem(k + 4 * i, N_BLK), p)
        return (k, lax.rem(p + 2 * i, N_DP))

    barrier = pltpu.get_barrier_semaphore()
    greeted = [(lax.rem(k + 2, N_BLK), p), (lax.rem(k - 2 + N_BLK, N_BLK), p), (pair, p), (skip, p)]
    for device in greeted:
        pl.semaphore_signal(barrier, inc=1, device_id=device, device_id_type=MESH)
    lead = 1 - core
    hub = lead * odd

    @pl.when(lead == 1)
    def _():
        pl.semaphore_signal(barrier, inc=1, device_id=group(1, 1), device_id_type=MESH)

    @pl.when(hub == 1)
    def _():
        for level in MIDDLE:
            for i in others(level):
                pl.semaphore_signal(barrier, inc=1, device_id=group(level, i), device_id_type=MESH)

    greetings = len(greeted) + lead + hub * sum(len(others(level)) for level in MIDDLE)

    def link(t):
        second = t // PIECES
        start = pl.multiple_of(PIECE * lax.rem(t, PIECES), PIECE)
        place = pl.multiple_of(2 * PIECE * t, PIECE)
        return pltpu.make_async_remote_copy(
            src_ref=unit.at[1 - second, pl.ds(start, PIECE)],
            dst_ref=held.at[pl.ds(place, PIECE)],
            send_sem=link_send.at[t],
            recv_sem=link_recv.at[t],
            device_id=(lax.rem(k + 2 - 4 * second + N_BLK, N_BLK), p),
            device_id_type=MESH,
        )

    def hand_on(t):
        place = pl.multiple_of(2 * PIECE * t, PIECE)
        return pltpu.make_async_remote_copy(
            src_ref=held.at[pl.ds(place, PIECE)],
            dst_ref=held.at[pl.ds(place + PIECE, PIECE)],
            send_sem=pass_send.at[t],
            recv_sem=pass_recv.at[t],
            device_id=(pair, p),
            device_id_type=MESH,
        )

    def to_pair(q):
        start = pl.multiple_of(TILE * q, TILE)
        return pltpu.make_async_remote_copy(
            src_ref=unit.at[1 - core, pl.ds(start, TILE)],
            dst_ref=held.at[pl.ds(PARTNER + start, TILE)],
            send_sem=pair_send.at[q],
            recv_sem=pair_recv.at[q],
            device_id=(pair, p),
            device_id_type=MESH,
        )

    def send_pair():
        for q in range(4):
            to_pair(q).start()

    def to_skip(q):
        start = pl.multiple_of(TILE * q, TILE)
        return pltpu.make_async_remote_copy(
            src_ref=unit.at[core, pl.ds(start, TILE)],
            dst_ref=held.at[pl.ds(SKIP + start, TILE)],
            send_sem=skip_send.at[q],
            recv_sem=skip_recv.at[q],
            device_id=(skip, p),
            device_id_type=MESH,
        )

    def normalize(side, j):
        rows = pl.ds(pl.multiple_of(PIECE * j, PIECE), PIECE)
        full = raw[side, rows, :].astype(F32)
        scaler = lax.rsqrt(jnp.sum(full * full, axis=-1, keepdims=True) + 1e-06)
        unit[side, rows, :] = (full * scaler).astype(BF16)
        factor[side, rows, :] = jnp.broadcast_to(scaler, (PIECE, 128))

    load_first.wait()
    normalize(1, 0)
    pl.semaphore_wait(barrier, greetings)
    link(0).start()
    load_rest.wait()

    @pl.loop(1, PIECES)
    def _(j):
        normalize(1, j)
        link(j).start()

    pl.when(core == 0)(send_pair)
    load(0).wait()

    @pl.loop(0, PIECES)
    def _(j):
        normalize(0, j)

    pl.when(core == 1)(send_pair)

    def send_skip():
        for q in range(4):
            to_skip(q).start()

    pl.when(odd * core == 0)(send_skip)

    @pl.when(odd == 1)
    def _():
        @pl.loop(PIECES, STEPS)
        def _(t):
            link(t).start()

    for copy in small:
        copy.wait()
    scale = jnp.exp(jnp.full((1, 128), log_scale[0], F32))
    shift = bias[0]
    sums[...] = jnp.zeros_like(sums)

    def count(weight, loss, logit, coeff):
        sums[0] += weight * fold(loss)
        sums[1] += weight * fold(logit)
        sums[2] += weight * fold(coeff)

    @pl.loop(0, ROWS // TILE)
    def _(c):
        cols = pl.ds(pl.multiple_of(TILE * c, TILE), TILE)
        rows = unit[0, cols, :]
        wanted = positives[:, cols]
        halves = []
        for h in range(2):
            part = pl.ds(HALF * h, HALF)
            product = scale * contract_last(unit[1, part, :], rows)
            logits = product + shift
            match = lax.broadcasted_iota(jnp.int32, (HALF, TILE), 0) + HALF * h == wanted
            odds = jnp.exp(jnp.where(match, -logits, logits))
            chance = odds / (1.0 + odds)
            coeff = jnp.where(match, -chance, chance)
            count(1.0, jnp.log1p(odds), coeff * product, coeff)
            coeff = coeff.astype(BF16)
            halves.append(coeff)
            term = jnp.dot(coeff, rows, preferred_element_type=F32)

            @pl.when(c == 0)
            def _():
                total[1, part, :] = term

            @pl.when(c > 0)
            def _():
                total[1, part, :] += term

        total[0, cols, :] = contract_first(jnp.concatenate(halves, axis=0), unit[1])

    def work_half(side, other, weight, h):
        part = pl.ds(HALF * h, HALF)
        product = scale * contract_last(unit[side, part, :], other)
        odds = jnp.exp(product + shift)
        coeff = odds / (1.0 + odds)
        if weight is not None:
            count(weight, jnp.log1p(odds), coeff * product, coeff)
        total[side, part, :] += jnp.dot(coeff.astype(BF16), other, preferred_element_type=F32)

    def work(side, place, weight):
        other = held[pl.ds(pl.multiple_of(place, TILE), TILE), :]
        for h in range(2):
            work_half(side, other, weight, h)

    lane = lax.broadcasted_iota(jnp.int32, (8, 128), 1)

    def exchange(level, i):
        return pltpu.make_async_remote_copy(
            src_ref=share.at[level, 0],
            dst_ref=share.at[level, i],
            send_sem=share_send.at[level, i - 1],
            recv_sem=share_recv.at[level, i - 1],
            device_id=group(level, i),
            device_id_type=MESH,
        )

    def gathered(level):
        for i in others(level):
            exchange(level, i).wait_recv()
        parts = [share[level, i] for i in range(len(others(level)) + 1)]
        while len(parts) > 1:
            half = len(parts) // 2
            parts = [parts[i] + parts[i + half] for i in range(half)]
        return parts[0]

    def send_share(level, value):
        share[level, 0] = value
        for i in others(level):
            exchange(level, i).start()

    def arrive(t):
        link(t).wait_recv()
        hand_on(t).start()

    def use(t, weight):
        hand_on(t).wait_recv()
        work(t // PIECES, 2 * PIECE * t, weight)

    ahead = (lax.rem(k + 2, N_BLK), p)

    @pl.loop(0, STEPS - 2)
    def _(t):
        arrive(t)

        @pl.when((odd == 0) & (t == PIECES - 2))
        def _():
            pl.semaphore_wait(go_sem, 1)

            @pl.loop(PIECES, STEPS)
            def _(i):
                link(i).start()

        pl.when((odd * core == 1) & (t == PIECES - 1))(send_skip)

        @pl.when((lead == 1) & (t == PIECES + 1))
        def _():
            share[1, 0] = gathered(0)
            pl.when(odd == 0)(lambda: exchange(1, 1).start())

        @pl.when(t > 0)
        def _():
            use(t - 1, jnp.where(t <= PIECES, 1.0, 0.0).astype(F32))

        @pl.when((odd == 1) & (t == PIECES - 2))
        def _():
            pl.semaphore_signal(go_sem, inc=1, device_id=ahead, device_id_type=MESH)

        second = t // PIECES
        q = t - 4 - 5 * second

        @pl.when((q >= 0) & (q < 4))
        def _():
            near = core == second
            pl.when(near)(lambda: to_pair(q).wait_recv())
            pl.when(jnp.logical_not(near))(lambda: to_skip(q).wait_recv())
            place = PARTNER + ROWS * (core + second - 2 * core * second)
            work(1 - second, place + TILE * q, 1.0 - second.astype(F32))

        @pl.when(t == PIECES)
        def _():
            value = jnp.zeros((8, 128), F32)
            for i in range(3):
                value = jnp.where(lane == i, jnp.sum(sums[i]), value)
            share[0, 0] = value
            pl.when(core == 1)(lambda: exchange(0, 1).start())

        for level in MIDDLE:
            @pl.when((hub == 1) & (t == PIECES - 1 + level))
            def _():
                send_share(level, gathered(level - 1))

        @pl.when((hub == 1) & (t == PIECES + 4))
        def _():
            value = gathered(4)
            send_share(5, value)
            send_share(6, value)

    def leave(side, j):
        rows = pl.ds(pl.multiple_of(PIECE * j, PIECE), PIECE)
        return pltpu.make_async_copy(
            result.at[side, rows], (image_grad, text_grad)[side].at[rows], out_sem.at[side, j]
        )

    def finish(side, j):
        rows = pl.ds(pl.multiple_of(PIECE * j, PIECE), PIECE)
        full = raw[side, rows, :].astype(F32)
        grad = total[side, rows, :]
        scaler = factor[side, rows, 0:1]
        inner = scaler * scaler * jnp.sum(full * grad, axis=-1, keepdims=True)
        result[side, rows, :] = (scale[:, 0:1] * scaler * (grad - full * inner)).astype(BF16)
        leave(side, j).start()

    arrive(STEPS - 2)
    use(STEPS - 3, None)

    @pl.loop(0, PIECES)
    def _(j):
        finish(0, j)

    use(STEPS - 2, None)

    for q in range(4):
        to_pair(q).wait_send()
        to_skip(q).wait_send()

    @pl.loop(0, STEPS - 2)
    def _(t):
        link(t).wait_send()
        hand_on(t).wait_send()

    @pl.loop(0, PIECES)
    def _(j):
        leave(0, j).wait()

    arrive(STEPS - 1)

    @pl.when((lead == 1) & (odd == 0))
    def _():
        exchange(5, 1).wait_recv()
        send_share(6, share[5, 1])

    hand_on(STEPS - 1).wait_recv()
    other = held[2 * PIECE * (STEPS - 1) : 2 * PIECE * STEPS, :]
    for h in range(2):
        work_half(1, other, None, h)
        for j in range(PIECES // 2):
            finish(1, PIECES // 2 * h + j)

    @pl.when(core == 1)
    def _():
        exchange(6, 1).wait_recv()
        share[6, 0] = share[6, 1]

    found = share[6, 0]
    for i in range(3):
        answer[i] = jnp.max(jnp.where(lane == i, found, -jnp.inf)) / COUNT
    leave_answer = pltpu.make_async_copy(answer, answer_out, answer_sem)
    leave_answer.start()
    pl.when(core == 1)(lambda: exchange(0, 1).wait_send())
    pl.when(lead == 1)(lambda: exchange(6, 1).wait_send())
    pl.when(lead * (1 - odd) == 1)(lambda: exchange(1, 1).wait_send())

    @pl.when(hub == 1)
    def _():
        for level in (*MIDDLE, 5):
            for i in others(level):
                exchange(level, i).wait_send()

    @pl.loop(STEPS - 2, STEPS)
    def _(t):
        link(t).wait_send()
        hand_on(t).wait_send()

    @pl.loop(0, PIECES)
    def _(j):
        leave(1, j).wait()

    leave_answer.wait()


def write(image, text, answer, image_grad, text_grad, totals, rows_held, totals_held, load_sem, store_sem):
    loads = [pltpu.make_async_copy(answer, totals_held, load_sem.at[2, 0])]
    stores = [pltpu.make_async_copy(totals_held, totals, store_sem.at[2, 0])]
    for i, (source, target) in enumerate(((image, image_grad), (text, text_grad))):
        for j in range(4):
            rows = pl.ds(TILE * j, TILE)
            loads.append(pltpu.make_async_copy(source.at[rows], rows_held.at[i, rows], load_sem.at[i, j]))
            stores.append(pltpu.make_async_copy(rows_held.at[i, rows], target.at[rows], store_sem.at[i, j]))
    for load in loads:
        load.start()
    for load, store in zip(loads, stores):
        load.wait()
        store.start()
    for store in stores:
        store.wait()


def body(images, texts, positives, log_scale, bias):
    hbm = pl.BlockSpec(memory_space=pltpu.HBM)
    dma = pltpu.SemaphoreType.DMA
    grad = jax.ShapeDtypeStruct((ROWS, WIDTH), BF16)
    three = jax.ShapeDtypeStruct((3,), F32)
    image, text, answer = pl.pallas_call(
        kernel,
        out_shape=(grad, grad, three),
        in_specs=[hbm, hbm, hbm, hbm, hbm],
        out_specs=(hbm, hbm, hbm),
        scratch_shapes=[
            pltpu.VMEM((1, ROWS), jnp.int32),
            pltpu.SMEM((1,), F32),
            pltpu.SMEM((1,), F32),
            pltpu.SMEM((3,), F32),
            pltpu.VMEM((2, ROWS, WIDTH), BF16),
            pltpu.VMEM((2, ROWS, WIDTH), BF16),
            pltpu.VMEM((2, ROWS, 128), F32),
            pltpu.VMEM((2, ROWS, WIDTH), F32),
            pltpu.VMEM((SKIP + ROWS, WIDTH), BF16),
            pltpu.VMEM((2, ROWS, WIDTH), BF16),
            pltpu.VMEM((3, 8, 128), F32),
            pltpu.VMEM((LEVELS, 8, 8, 128), F32),
            dma((6,)),
            dma((STEPS,)),
            dma((STEPS,)),
            dma((STEPS,)),
            dma((STEPS,)),
            dma((4,)),
            dma((4,)),
            dma((4,)),
            dma((4,)),
            dma((LEVELS, 7)),
            dma((LEVELS, 7)),
            dma((2, PIECES)),
            dma,
            pltpu.SemaphoreType.REGULAR,
        ],
        compiler_params=pltpu.CompilerParams(
            collective_id=0, has_side_effects=True, vmem_limit_bytes=58 << 20
        ),
        cost_estimate=pl.CostEstimate(
            flops=15 * 2 * ROWS * ROWS * WIDTH, bytes_accessed=4 * ROWS * WIDTH * 2, transcendentals=0
        ),
    )(images, texts, positives, log_scale, bias)
    return pl.pallas_call(
        write,
        out_shape=(grad, grad, three),
        in_specs=[hbm, hbm, hbm],
        out_specs=(hbm, hbm, hbm),
        scratch_shapes=[
            pltpu.VMEM((2, ROWS, WIDTH), BF16),
            pltpu.SMEM((3,), F32),
            dma((3, 4)),
            dma((3, 4)),
        ],
        compiler_params=pltpu.CompilerParams(vmem_limit_bytes=60 << 20),
    )(image, text, answer)


def solution(mesh):
    return jax.shard_map(
        body,
        mesh=mesh,
        in_specs=(P(("blk", "dp"), None), P(("blk", "dp"), None), P(("blk", "dp"), None), P(), P()),
        out_specs=(P(("blk", "dp"), None), P(("blk", "dp"), None), P()),
        check_vma=False,
    )
```
